256 devices in a mesh: role: 2 (over y_lo), proto: 64 (over x, y_hi, z), crop: 2 (over core).
Axes of the slice: x: 4, y: 4 (y_hi: 2, y_lo: 2; y = y_hi * 2 + y_lo), z: 8, core: 2. Of those that a mesh axis runs over, the one named last changes fastest.
Arguments:
- embeddings: bfloat16 [2, 1024, 512], P('role', 'crop'), may hold values from -1 to 1, as said below
- weights: bfloat16 [2, 512, 262144], P('role', None, 'proto'), may hold values from -1 to 1, as said below
Outputs:
- weight_grad: bfloat16 [2, 2, 128, 262144], P('crop', 'role', None, 'proto')
- embed_grad: bfloat16 [2, 512, 512], P('crop', 'proto', 'role')
The draws below stay inside these ranges and needn't reach their ends.
Inputs may be any that keep to these rules, and one draw needn't show every extreme that they name: `embeddings`: each crop's row has unit Euclidean length before rounding to bfloat16. `weights`: each prototype column has unit Euclidean length before rounding to bfloat16.
All inputs are finite; a program needn't handle non-finite values.
Results may differ from the reference program's by a relative error of at most 0.001.
The reference program's roundings to bfloat16 on the way (of `targets` and `logit_grads`) count: a program that leaves them out, or rounds other values in their place, can miss the bound.
Values may be sent and summed in bfloat16 or wider, within the bound.
A program may use at most 128 MiB of HBM per device.

```python
import jax
import jax.numpy as jnp
from jax import lax

D = 512
PROTOS = 262144
CROPS = 1024
ITERS = 3


cluster_count = 4


def unit_rows(values):
    return values / jnp.sqrt(jnp.sum(values * values, axis=1, keepdims=True))


def rough_rows(row_key, row_total):
    values = jax.random.normal(row_key, (row_total, D), jnp.float32)
    return unit_rows(values)


def group_centers(key, which_group):
    centers = jax.random.normal(jax.random.fold_in(key, 71 + which_group), (cluster_count, D), jnp.float32)
    return unit_rows(centers)


def draw_weights(key, part):
    matrices = []
    for which_group in range(2):
        centers = group_centers(key, which_group)
        member = jax.random.randint(jax.random.fold_in(key, 31 + which_group), (PROTOS,), 0, cluster_count, jnp.int32)
        columns = rough_rows(jax.random.fold_in(key, 61 + which_group), PROTOS)
        toward = jnp.take(centers, member, axis=0)
        columns = columns + 0.8 * toward
        matrices.append(unit_rows(columns).T.astype(jnp.bfloat16))
    return jnp.stack(matrices)


def draw_embeddings(key, part):
    groups = []
    for which_group in range(2):
        centers = group_centers(key, which_group)
        member = jnp.maximum(jax.random.randint(jax.random.fold_in(key, 41 + which_group), (CROPS,), -cluster_count, cluster_count, jnp.int32), 0)
        toward = jnp.take(centers, member, axis=0)
        noise = rough_rows(jax.random.fold_in(key, 51 + which_group), CROPS)
        mixed = 0.5 * toward + 0.866 * noise
        groups.append(unit_rows(mixed))
    return jnp.stack(groups).astype(jnp.bfloat16)


def setup_inputs(seed: int = 0) -> dict:
    key_of = jax.random.split(jax.random.key(seed), 3)
    embeddings = draw_embeddings(jax.random.fold_in(key_of[2], 71), 0)
    weights = draw_weights(jax.random.fold_in(key_of[2], 71), 0)
    return dict(embeddings=embeddings, weights=weights)


def log_sum(numeric_items, along):
    return jnp.log(jnp.sum(jnp.exp(numeric_items), axis=along, keepdims=True))


def reference(embeddings, weights):
    teacher_scores = jnp.dot(embeddings[0], weights[0], preferred_element_type=jnp.float32)
    student_scores = jnp.dot(embeddings[1], weights[1], preferred_element_type=jnp.float32)
    teacher_logits = teacher_scores / 0.07
    student_logits = student_scores / 0.1
    row_shift = jnp.zeros((CROPS, 1), jnp.float32)
    column_shift = jnp.zeros((1, PROTOS), jnp.float32)
    for iteration in range(ITERS):
        column_shift = -log_sum(teacher_logits + row_shift, 0)
        row_shift = -log_sum(teacher_logits + column_shift, 1)
    targets = jnp.exp(teacher_logits + column_shift + row_shift).astype(jnp.bfloat16)
    student_exp = jnp.exp(student_logits)
    student_probs = student_exp / jnp.sum(student_exp, axis=1, keepdims=True)
    logit_grads = ((student_probs - targets.astype(jnp.float32)) / 0.1).astype(jnp.bfloat16)
    weight_full = lax.dot_general(embeddings[1], logit_grads, (((0,), (0,)), ((), ())), preferred_element_type=jnp.float32)
    embed_full = lax.dot_general(logit_grads, weights[1], (((1,), (1,)), ((), ())), preferred_element_type=jnp.float32)
    weight_grad = weight_full.astype(jnp.bfloat16).reshape(2, 2, D // 4, PROTOS)
    embed_grad = embed_full.astype(jnp.bfloat16).reshape(2, CROPS // 2, D)
    return weight_grad, embed_grad
```

```python
import functools

import jax
import jax.numpy as jnp
from jax import lax
from jax.experimental import pallas as pl
from jax.experimental.pallas import tpu as pltpu
from jax.sharding import PartitionSpec as P

F32 = jnp.float32
BF16 = jnp.bfloat16
MESH = pl.DeviceIdType.MESH
LANES = 128
TILE = 256
CHIPS = {64: (4, 2, 8), 8: (2, 2, 2), 4: (2, 2, 1)}
R1, R2, R3, SINV = range(4)


def across(column, width):
    return jnp.concatenate([column] * (width // LANES), axis=1)


def kernel(chips, emb, wgt, wg_out, eg_out,
           EB, WB, AB, G, ET, U, RS, COL, SRC1, SRC2, AR1, AR2, MSRC, MSG,
           EGP, RC, RX, S1, RZ, S2, RY, WGB,
           loc, e_send, e_recv, w_send, w_recv, a1s, a1r, a2s, a2r, m_send, m_recv,
           c_send, c_recv, x_send, x_recv, z_send, z_recv, y_send, y_recv, g_send, g_recv, g_loc):
    nx, nyh, nz = chips
    role, p, c = (lax.axis_index(a) for a in ("role", "proto", "crop"))
    x, yh, z = p // (nyh * nz), (p // nz) % nyh, p % nz
    teacher = role == 0
    half, D = emb.shape[1], emb.shape[2]
    B = 2 * half
    PC = wgt.shape[2] // 2
    PG = PC // 2
    vrows = B // LANES
    owned = half // p_count(chips)
    quarter = D // 4

    def at(role_, x_, yh_, z_, c_):
        return {"role": role_, "proto": (x_ * nyh + yh_) * nz + z_, "crop": c_}

    def send(src, dst, s, r, to):
        copy = pltpu.make_async_remote_copy(
            src_ref=src, dst_ref=dst, send_sem=s, recv_sem=r, device_id=to, device_id_type=MESH)
        copy.start()
        return copy

    def arrived(ref, sem):
        pltpu.make_async_copy(ref, ref, sem).wait()

    other_core = at(role, x, yh, z, 1 - c)
    partner = at(1 - role, x, yh, z, c)
    wrap = at(1 - role, x, 1 - yh, z, c)

    n1, n2 = 2 * nz, nx * nyh
    id1, id2 = 2 * z + c, x * nyh + yh

    def peer1(d):
        j = (id1 + d) % n1
        return at(role, x, yh, j // 2, j % 2)

    def peer2(d):
        j = (id2 + d) % n2
        return at(role, j // nyh, j % nyh, z, c)

    barrier = pltpu.get_barrier_semaphore()

    def greet(to):
        pl.semaphore_signal(barrier, inc=1, device_id=to, device_id_type=MESH)

    for d in range(1, n1):
        greet(peer1(d))
    for d in range(1, n2):
        greet(peer2(d))
    greet(partner)
    greet(at(1 - role, x, yh, z, 1 - c))
    greet(wrap)
    own_e = pltpu.make_async_copy(emb.at[0], EB.at[role, pl.ds(pl.multiple_of(c * half, half), half)], loc.at[0])
    own_e.start()
    own_w = pltpu.make_async_copy(
        wgt.at[0, :, pl.ds(pl.multiple_of(c * PC, PC), PC)], WB.at[role], loc.at[1])
    own_w.start()
    pl.semaphore_wait(barrier, n1 - 1 + n2 - 1 + 3)

    my_half = pl.ds(pl.multiple_of(c * half, half), half)
    e_core = send(emb.at[0], EB.at[role, my_half], e_send.at[0], e_recv.at[0], other_core)
    e_wrap = send(emb.at[0], EB.at[role, my_half], e_send.at[1], e_recv.at[1], wrap)
    away = pl.multiple_of((1 - role) * PG, PG)
    w_swap = send(
        wgt.at[0, :, pl.ds(pl.multiple_of(c * PC + (1 - role) * PG, PG), PG)],
        WB.at[role, :, pl.ds(away, PG)], w_send.at[0], w_recv.at[0], partner)

    gcols = pl.ds(pl.multiple_of(role * PG, PG), PG)
    inv_t, inv_s = 1.0 / 0.07, 1.0 / 0.1
    scale = jnp.where(teacher, inv_t, inv_s).astype(F32)
    other_scale = jnp.where(teacher, inv_s, inv_t).astype(F32)

    def expand(ref, slot):
        for i in range(vrows):
            COL[slot, i * LANES:(i + 1) * LANES, :] = jnp.broadcast_to(
                ref[i:i + 1, :], (LANES, LANES)).T

    def shrink(it):
        for i in range(vrows):
            SRC1[it, i:i + 1, :] = jnp.sum(
                RS[i * LANES:(i + 1) * LANES, :].T, axis=0, keepdims=True)

    def stage1(it):
        shrink(it)

        def one(d, _):
            send(SRC1.at[it], AR1.at[it, d - 1], a1s.at[it], a1r.at[it], peer1(d))
            return 0

        lax.fori_loop(1, n1, one, 0)

    def stage2(it):
        arrived(AR1.at[it], a1r.at[it])
        total = SRC1[it]
        for d in range(n1 - 1):
            total = total + AR1[it, d]
        SRC2[it] = total

        def one(d, _):
            send(SRC2.at[it], AR2.at[it, d - 1], a2s.at[it], a2r.at[it], peer2(d))
            return 0

        lax.fori_loop(1, n2, one, 0)

    def finish(it):
        arrived(AR2.at[it], a2r.at[it])
        total = SRC2[it]
        for d in range(n2 - 1):
            total = total + AR2[it, d]
        MSRC[it] = 1.0 / total

    def column_scales(slot, cols, width):
        def body(i, acc):
            for k in range(4):
                rows = pl.ds(pl.multiple_of(i * 32 + k * 8, 8), 8)
                acc = acc + AB[0, rows, cols] * across(COL[slot, rows, :], width)
            return acc

        acc = lax.fori_loop(0, B // 32, body, jnp.zeros((8, width), F32))
        u = 1.0 / jnp.sum(acc, axis=0, keepdims=True)
        U[:, cols] = u
        return u

    def row_parts(u):
        ub = jnp.broadcast_to(u, (8, PC))

        def body(i, _):
            for k in range(4):
                rows = pl.ds(pl.multiple_of(i * 32 + k * 8, 8), 8)
                m = AB[0, rows, :] * ub
                acc = m[:, :LANES]
                for l in range(1, PC // LANES):
                    acc = acc + m[:, l * LANES:(l + 1) * LANES]
                RS[rows, :] = acc
            return 0

        lax.fori_loop(0, B // 32, body, 0)

    fwd_half = my_half

    def forward():
        arrived(EB.at[1 - role, my_half], e_recv.at[1])
        send(EB.at[1 - role, fwd_half], EB.at[1 - role, fwd_half], e_send.at[2], e_recv.at[2], other_core)

    def other_role():
        arrived(EB.at[1 - role, my_half], e_recv.at[2])
        arrived(WB.at[1 - role, :, gcols], w_recv.at[0])
        for i in range(B // TILE):
            ET[:, i * TILE:(i + 1) * TILE] = EB[1, i * TILE:(i + 1) * TILE, :].T

        def tile(j, _):
            cols = pl.ds(pl.multiple_of(role * PG + j * TILE, TILE), TILE)
            s = jnp.dot(EB[1 - role], WB[1 - role, :, cols], preferred_element_type=F32)
            AB[1 - role, :, cols] = jnp.exp(s * other_scale)
            return 0

        lax.fori_loop(0, PG // TILE, tile, 0)

    own_e.wait()
    own_w.wait()
    arrived(EB.at[role, my_half], e_recv.at[0])
    RS[...] = jnp.zeros_like(RS)

    def own_tile(j, _):
        cols = pl.ds(pl.multiple_of(j * TILE, TILE), TILE)
        s = jnp.dot(EB[role], WB[role, :, cols], preferred_element_type=F32)
        a = jnp.exp(s * scale)
        AB[role, :, cols] = a
        u = jnp.where(teacher, 1.0 / jnp.sum(a, axis=0, keepdims=True), 1.0)
        acc = RS[...]
        for l in range(TILE // LANES):
            acc = acc + a[:, l * LANES:(l + 1) * LANES] * u[:, l * LANES:(l + 1) * LANES]
        RS[...] = acc
        return 0

    lax.fori_loop(0, PC // TILE, own_tile, 0)
    stage1(0)
    stage2(0)
    finish(0)

    @pl.when(teacher)
    def _():
        expand(MSRC.at[0], R1)
        row_parts(column_scales(R1, slice(None), PC))
        stage1(1)
        forward()
        stage2(1)
        finish(1)
        send(MSRC.at[1], MSG.at[1], m_send.at[1], m_recv.at[1], partner)
        expand(MSRC.at[1], R2)
        row_parts(column_scales(R2, slice(None), PC))
        stage1(2)
        stage2(2)
        other_role()
        arrived(MSG.at[0], m_recv.at[0])
        expand(MSG.at[0], SINV)
        finish(2)
        send(MSRC.at[2], MSG.at[2], m_send.at[2], m_recv.at[2], partner)
        expand(MSRC.at[2], R3)

    @pl.when(jnp.logical_not(teacher))
    def _():
        send(MSRC.at[0], MSG.at[0], m_send.at[0], m_recv.at[0], partner)
        expand(MSRC.at[0], SINV)
        forward()
        other_role()
        arrived(MSG.at[1], m_recv.at[1])
        expand(MSG.at[1], R2)
        column_scales(R2, gcols, PG)
        arrived(MSG.at[2], m_recv.at[2])
        expand(MSG.at[2], R3)

    xrows = half // nx

    def block(h, xb):
        start = pl.multiple_of(h * half + xb * xrows, xrows)

        def body(i, _):
            rows = pl.ds(pl.multiple_of(start + i * 16, 16), 16)
            t = AB[0, rows, gcols] * U[:, gcols] * across(COL[R3, rows, :], PG)
            s = AB[1, rows, gcols] * across(COL[SINV, rows, :], PG)
            G[rows, :] = ((s - t.astype(BF16).astype(F32)) * 10.0).astype(BF16)
            return 0

        lax.fori_loop(0, xrows // 16, body, 0)
        EGP[h, pl.ds(pl.multiple_of(xb * xrows, xrows), xrows), :] = lax.dot_general(
            G[pl.ds(start, xrows), :], WB[1, :, gcols], (((1,), (1,)), ((), ())),
            preferred_element_type=F32)

    def chunk(d):
        xb = (x + 1 + d) % nx
        return xb, pl.ds(pl.multiple_of(xb * xrows, xrows), xrows)

    def core_sum(d):
        xb, rows = chunk(d)
        arrived(RC.at[rows], c_recv.at[d])
        EGP[c, rows, :] = EGP[c, rows, :] + RC[rows, :]

    def x_step(d, _):
        xb, rows = chunk(d)
        block(1 - c, xb)
        send(EGP.at[1 - c, rows], RC.at[rows], c_send.at[d], c_recv.at[d], other_core)
        block(c, xb)
        core_sum(d)

        @pl.when(d < nx - 1)
        def _():
            send(EGP.at[c, rows], RX.at[d], x_send.at[d], x_recv.at[d], at(role, xb, yh, z, c))
        return 0

    lax.fori_loop(0, nx, x_step, 0)

    my_q = 2 * c + role

    def wg_tile(j, _):
        cols = pl.ds(pl.multiple_of(j * TILE, TILE), TILE)
        WGB[:, cols] = jnp.dot(ET[...], G[:, cols], preferred_element_type=F32).astype(BF16)
        dst = wg_out.at[0, 0, :, pl.ds(pl.multiple_of(c * PC + role * PG + j * TILE, TILE), TILE)]
        for d in range(1, 4):
            q = (my_q + d) % 4
            src = WGB.at[pl.ds(pl.multiple_of(q * quarter, quarter), quarter), cols]
            send(src, dst, g_send.at[0], g_recv.at[0], at(q % 2, x, yh, z, q // 2))
        return 0

    lax.fori_loop(0, PG // TILE, wg_tile, 0)
    mine = pltpu.make_async_copy(
        WGB.at[pl.ds(pl.multiple_of(my_q * quarter, quarter), quarter)],
        wg_out.at[0, 0, :, pl.ds(pl.multiple_of(c * PC + role * PG, PG), PG)], g_loc.at[0])
    mine.start()

    _, own_rows = chunk(nx - 1)
    total = EGP[c, own_rows, :]
    for d in range(nx - 1):
        arrived(RX.at[d], x_recv.at[d])
        total = total + RX[d]
    S1[...] = total.reshape(S1.shape)
    if nz > 1:
        for d in range(1, nz):
            zz = (z + d) % nz
            send(S1.at[:, zz], RZ.at[d - 1], z_send.at[0], z_recv.at[0], at(role, x, yh, zz, c))
        arrived(RZ, z_recv.at[0])
    part = S1[:, z]
    for d in range(nz - 1):
        part = part + RZ[d]
    for g in range(2):
        S2[g] = part[:, :, g * (D // 2):(g + 1) * (D // 2)]
    my_y = 2 * yh + role
    for d in range(1, 2 * nyh):
        j = (my_y + d) % (2 * nyh)
        send(S2.at[j % 2, j // 2], RY.at[d - 1], y_send.at[0], y_recv.at[0], at(j % 2, x, j // 2, z, c))
    arrived(RY, y_recv.at[0])
    out = S2[role, yh]
    for d in range(2 * nyh - 1):
        out = out + RY[d]
    eg_out[...] = out

    e_core.wait_send()
    e_wrap.wait_send()
    arrived(EB.at[role, my_half], e_send.at[2])
    w_swap.wait_send()

    def sent(it):
        arrived(AR1.at[it], a1s.at[it])
        arrived(AR2.at[it], a2s.at[it])

    sent(0)

    @pl.when(teacher)
    def _():
        sent(1)
        sent(2)
        arrived(MSG.at[1], m_send.at[1])
        arrived(MSG.at[2], m_send.at[2])

    @pl.when(jnp.logical_not(teacher))
    def _():
        arrived(MSG.at[0], m_send.at[0])

    for d in range(nx):
        arrived(RC.at[pl.ds(0, xrows)], c_send.at[d])
    for d in range(nx - 1):
        arrived(RX.at[d], x_send.at[d])
    if nz > 1:
        arrived(RZ, z_send.at[0])
    arrived(RY, y_send.at[0])
    three = wg_out.at[0, 0, :, pl.ds(0, 3 * PG)]
    arrived(three, g_recv.at[0])
    arrived(three, g_send.at[0])
    mine.wait()


def p_count(chips):
    return chips[0] * chips[1] * chips[2]


def solution(mesh):
    chips = CHIPS[mesh.shape["proto"]]
    nx, nyh, nz = chips

    def per_device(emb, wgt):
        half, D = emb.shape[1:]
        B, PC = 2 * half, wgt.shape[2] // 2
        PG = PC // 2
        vrows, owned, xrows = B // LANES, half // p_count(chips), half // nx
        dma = pltpu.SemaphoreType.DMA
        wg, eg = pl.pallas_call(
            functools.partial(kernel, chips),
            name="head_step",
            out_shape=(
                jax.ShapeDtypeStruct((1, 1, D // 4, 2 * PC), BF16),
                jax.ShapeDtypeStruct((owned, D // 2), F32),
            ),
            in_specs=[pl.BlockSpec(memory_space=pl.ANY)] * 2,
            out_specs=(pl.BlockSpec(memory_space=pl.ANY), pl.BlockSpec(memory_space=pltpu.VMEM)),
            scratch_shapes=[
                pltpu.VMEM((2, B, D), BF16),
                pltpu.VMEM((2, D, PC), BF16),
                pltpu.VMEM((2, B, PC), F32),
                pltpu.VMEM((B, PG), BF16),
                pltpu.VMEM((D, B), BF16),
                pltpu.VMEM((1, PC), F32),
                pltpu.VMEM((B, LANES), F32),
                pltpu.VMEM((4, B, LANES), F32),
                pltpu.VMEM((3, vrows, LANES), F32),
                pltpu.VMEM((3, vrows, LANES), F32),
                pltpu.VMEM((3, 2 * nz - 1, vrows, LANES), F32),
                pltpu.VMEM((3, nx * nyh - 1, vrows, LANES), F32),
                pltpu.VMEM((3, vrows, LANES), F32),
                pltpu.VMEM((3, vrows, LANES), F32),
                pltpu.VMEM((2, half, D), F32),
                pltpu.VMEM((half, D), F32),
                pltpu.VMEM((max(nx - 1, 1), xrows, D), F32),
                pltpu.VMEM((nyh, nz, owned, D), F32),
                pltpu.VMEM((max(nz - 1, 1), nyh, owned, D), F32),
                pltpu.VMEM((2, nyh, owned, D // 2), F32),
                pltpu.VMEM((2 * nyh - 1, owned, D // 2), F32),
                pltpu.VMEM((D, PG), BF16),
                dma((2,)), dma((3,)), dma((3,)), dma((1,)), dma((1,)),
                dma((3,)), dma((3,)), dma((3,)), dma((3,)), dma((3,)), dma((3,)),
                dma((nx,)), dma((nx,)), dma((nx,)), dma((nx,)),
                dma((1,)), dma((1,)), dma((1,)), dma((1,)), dma((1,)), dma((1,)), dma((1,)),
            ],
            compiler_params=pltpu.CompilerParams(
                collective_id=0, has_side_effects=True, vmem_limit_bytes=56 * 1024 * 1024),
            cost_estimate=pl.CostEstimate(
                flops=2 * B * D * PG * 5, bytes_accessed=8 * D * PC, transcendentals=3 * B * PG),
        )(emb, wgt)
        return wg, eg.astype(BF16)[None]

    return jax.shard_map(
        per_device,
        mesh=mesh,
        in_specs=(P("role", "crop", None), P("role", None, "proto")),
        out_specs=(P("crop", "role", None, "proto"), P("crop", "proto", "role")),
        check_vma=False,
    )
```

```python
import functools

import jax
import jax.numpy as jnp
from jax import lax
from jax.experimental import pallas as pl
from jax.experimental.pallas import tpu as pltpu
from jax.sharding import PartitionSpec as P

F32 = jnp.float32
BF16 = jnp.bfloat16
MESH = pl.DeviceIdType.MESH
LANES = 128
TILE = 256
CHIPS = {64: (4, 2, 8), 8: (2, 2, 2), 4: (2, 2, 1)}
BATCHES = (5, 6, 5)


def across(column, width):
    return jnp.concatenate([column] * (width // LANES), axis=1)


def far_first(n):
    return sorted(range(1, n), key=lambda m: -max(min(abs(a - (a ^ m)), n - abs(a - (a ^ m))) for a in range(n)))


def kernel(chips, emb, wgt, wg_out, eg_out,
           EB, WO, WX, KC, AB, G, ET, WT, PCS, PCR, UT, UG, RS, COLR, COLS, COL3,
           SRC1, SRC2, AR1, AR2, AR2S, RV, SV, R3V, EGP, RC, RX, S1, RZ, S2, RY, WGB,
           loc, w_loc, e_send, e_recv, w_send, w_recv, p_send, p_recv, a1s, a1r, a2s, a2r, b_send, b_recv,
           u_send, u_recv, v_send, v_recv, r_send, r_recv, c_send, c_recv, x_send, x_recv,
           z_send, z_recv, y_send, y_recv, g_send, g_recv, g_loc):
    nx, nyh, nz = chips
    role, p, c = (lax.axis_index(a) for a in ("role", "proto", "crop"))
    x, yh, z = p // (nyh * nz), (p // nz) % nyh, p % nz
    teacher = role == 0
    student = role == 1
    half, D = emb.shape[1], emb.shape[2]
    B = 2 * half
    PB = wgt.shape[2]
    PC, PG = PB // 2, PB // 4
    vrows = half // LANES
    crows, grows = PC // LANES, PG // LANES
    quarter = D // 4

    def at(mr=0, mx=0, my=0, mz=0, mc=0):
        return {"role": role ^ mr, "proto": p ^ ((mx * nyh + my) * nz + mz), "crop": c ^ mc}

    def send(src, dst, s, r, to):
        pltpu.make_async_remote_copy(
            src_ref=src, dst_ref=dst, send_sem=s, recv_sem=r, device_id=to, device_id_type=MESH).start()

    def arrived(ref, sem):
        pltpu.make_async_copy(ref, ref, sem).wait()

    z_peers = far_first(nz)
    x_peers = far_first(nx)
    xy_peers = sorted(range(1, nx * nyh), key=lambda m: -((m // nyh in (1, 3)) + 2 * (m // nyh == 2) + 2 * (m % nyh)))

    barrier = pltpu.get_barrier_semaphore()
    greeted = [at(mz=m) for m in z_peers] + [at(mx=m // nyh, my=m % nyh) for m in xy_peers]
    greeted += [at(mr=1, mx=m // nyh, my=m % nyh) for m in range(nx * nyh)] + [at(mc=1), at(mr=1, mc=1)]
    for to in greeted:
        pl.semaphore_signal(barrier, inc=1, device_id=to, device_id_type=MESH)

    my_half = pl.ds(pl.multiple_of(c * half, half), half)
    own_e = pltpu.make_async_copy(emb.at[0], EB.at[role, my_half], loc.at[0])
    own_e.start()
    own_w = []
    for k in range(4):
        cols = pl.ds(k * PG, PG)
        own_w.append(pltpu.make_async_copy(wgt.at[0, :, cols], WO.at[:, cols], w_loc.at[k]))
        own_w[-1].start()

    inv_t, inv_s = 1.0 / 0.07, 1.0 / 0.1
    scale = jnp.where(teacher, inv_t, inv_s).astype(F32)

    own_e.wait()
    for k in range(4):
        own_w[k].wait()

        def own_tile(j, _, k=k):
            cols = pl.ds(pl.multiple_of(k * PG + j * TILE, TILE), TILE)
            s = jnp.dot(EB[role, my_half, :], WO[:, cols], preferred_element_type=F32)
            a = jnp.exp(s * scale)
            KC[:, cols] = a
            cs = jnp.sum(a, axis=0, keepdims=True)
            for l in range(TILE // LANES):
                PCS[0, k // 2, pl.ds((k % 2) * grows + j * (TILE // LANES) + l, 1), :] = cs[:, l * LANES:(l + 1) * LANES]
            return 0

        lax.fori_loop(0, PG // TILE, own_tile, 0)

    pl.semaphore_wait(barrier, len(greeted))

    g_own = pl.multiple_of(c * PC + role * PG, PG)
    g_away = pl.multiple_of(c * PC + (1 - role) * PG, PG)
    step_rows = D // sum(BATCHES)

    def send_columns(it, h):
        send(PCS.at[it, h], PCR.at[it, h], p_send.at[it, h], p_recv.at[it, h], at(mc=1))

    def send_core():
        send(emb.at[0], EB.at[role, my_half], e_send.at[0], e_recv.at[0], at(mc=1))

    def send_wrap(h):
        rows = pl.ds(h * (half // 2), half // 2)
        there = pl.ds(pl.multiple_of(c * half + h * (half // 2), half // 2), half // 2)
        send(emb.at[0, rows], EB.at[role, there], e_send.at[1], e_recv.at[1], at(mr=1, my=1))

    def send_weights(k):
        for q in range(sum(BATCHES[:k]), sum(BATCHES[:k + 1])):
            rows = pl.ds(q * step_rows, step_rows)
            send(wgt.at[0, rows, pl.ds(g_away, PG)], WX.at[rows, :], w_send.at[0], w_recv.at[0], at(mr=1))

    def expand(vec, ref, first=0):
        for i in range(vrows):
            rows = pl.ds(pl.multiple_of(first + i * LANES, LANES), LANES)
            ref[rows, :] = jnp.broadcast_to(vec[i:i + 1, :], (LANES, LANES)).T

    def column_parts(it, h):
        def body(i, acc):
            for k in range(4):
                rows = pl.ds(pl.multiple_of(i * 32 + k * 8, 8), 8)
                acc = acc + KC[rows, h * PC:(h + 1) * PC] * across(COLR[rows, :], PC)
            return acc

        acc = lax.fori_loop(0, half // 32, body, jnp.zeros((8, PC), F32))
        cs = jnp.sum(acc, axis=0, keepdims=True)
        for l in range(crows):
            PCS[it, h, l:l + 1, :] = cs[:, l * LANES:(l + 1) * LANES]
        send_columns(it, h)

    def column_scales(it, h):
        arrived(PCR.at[it, h], p_recv.at[it, h])
        UT[h] = 1.0 / (PCS[it, h] + PCR[it, h])

    def row_parts(h):
        ub = jnp.concatenate(
            [jnp.broadcast_to(UT[h, l:l + 1, :], (8, LANES)) for l in range(crows)], axis=1)

        def body(i, _):
            for k in range(4):
                rows = pl.ds(pl.multiple_of(i * 32 + k * 8, 8), 8)
                m = KC[rows, h * PC:(h + 1) * PC] * ub
                parts = [m[:, l * LANES:(l + 1) * LANES] for l in range(crows)]
                while len(parts) > 1:
                    parts = [a + b for a, b in zip(parts[::2], parts[1::2])]
                RS[rows, :] = parts[0] if h == 0 else RS[rows, :] + parts[0]
            return 0

        lax.fori_loop(0, half // 32, body, 0)

    def stage1(it):
        for i in range(vrows):
            SRC1[it, i:i + 1, :] = jnp.sum(RS[i * LANES:(i + 1) * LANES, :].T, axis=0, keepdims=True)
        for m in z_peers:
            send(SRC1.at[it], AR1.at[it, m - 1], a1s.at[it], a1r.at[it], at(mz=m))

    def stage2(it):
        total = SRC1[it]
        if nz > 1:
            arrived(AR1.at[it], a1r.at[it])
            for m in range(nz - 1):
                total = total + AR1[it, m]
        SRC2[it] = total
        for m in xy_peers:
            send(SRC2.at[it], AR2.at[it, m - 1], a2s.at[it], a2r.at[it], at(mx=m // nyh, my=m % nyh))
        if it == 2:
            for m in range(nx * nyh):
                send(SRC2.at[it], AR2S.at[m], b_send.at[0], b_recv.at[0], at(mr=1, mx=m // nyh, my=m % nyh))

    def finish(it):
        arrived(AR2.at[it], a2r.at[it])
        total = SRC2[it]
        for m in range(nx * nyh - 1):
            total = total + AR2[it, m]
        return 1.0 / total

    def forward():
        arrived(EB.at[1 - role, my_half], e_recv.at[1])
        send(EB.at[1 - role, my_half], EB.at[1 - role, my_half], e_send.at[2], e_recv.at[2], at(mc=1))

    def exps(which, weights, first, inv, scaled):
        def tile(j, _):
            cols = pl.ds(pl.multiple_of(j * TILE, TILE), TILE)
            w_cols = pl.ds(pl.multiple_of(first + j * TILE, TILE), TILE)
            s = jnp.dot(EB[which], weights[:, w_cols], preferred_element_type=F32)
            a = jnp.exp(s * inv)
            AB[which, :, cols] = a * across(COLS[...], TILE) if scaled else a
            return 0

        lax.fori_loop(0, PG // TILE, tile, 0)

    def scale_targets():
        ub = jnp.concatenate(
            [jnp.broadcast_to(UG[l:l + 1, :], (8, LANES)) for l in range(grows)], axis=1)

        def body(i, _):
            for k in range(4):
                rows = pl.ds(pl.multiple_of(i * 32 + k * 8, 8), 8)
                AB[0, rows, :] = AB[0, rows, :] * ub
            return 0

        lax.fori_loop(0, B // 32, body, 0)

    def turn_student(weights, first):
        for i in range(B // TILE):
            ET[:, i * TILE:(i + 1) * TILE] = EB[1, i * TILE:(i + 1) * TILE, :].T

        def body(i, _):
            rows = pl.ds(pl.multiple_of(i * TILE, TILE), TILE)
            WT[rows, :] = weights[:, pl.ds(pl.multiple_of(first + i * TILE, TILE), TILE)].T
            return 0

        lax.fori_loop(0, PG // TILE, body, 0)

    @pl.when(teacher)
    def _():
        for h in range(2):
            send_columns(0, h)
        send_core()
        send_wrap(0)
        send_wrap(1)
        send_weights(0)
        for h in range(2):
            column_scales(0, h)
            row_parts(h)
        stage1(0)
        arrived(EB.at[role, my_half], e_recv.at[0])
        exps(0, WO, g_own, inv_t, False)
        stage2(0)
        r = finish(0)
        for it in (1, 2):
            expand(r, COLR)
            send_weights(it)
            for h in range(2):
                column_parts(it, h)
            for h in range(2):
                column_scales(it, h)
                row_parts(h)
            stage1(it)
            if it == 1:
                forward()
            else:
                UG[...] = UT[c, 0:grows, :]
                send(UT.at[c, pl.ds(grows, grows)], UG, u_send.at[0], u_recv.at[0], at(mr=1))
                scale_targets()
                arrived(EB.at[1 - role, my_half], e_recv.at[2])
                arrived(WX, w_recv.at[0])
                turn_student(WX, 0)
            stage2(it)
            if it == 2:
                arrived(SV.at[c], v_recv.at[1])
                arrived(SV.at[1 - c], v_recv.at[2])
                for h in range(2):
                    expand(SV[h], COLS, h * half)
                exps(1, WX, 0, inv_s, True)
            r = finish(it)
        R3V[c] = r

    @pl.when(student)
    def _():
        send_core()
        send_wrap(0)
        for k in range(len(BATCHES)):
            send_weights(k)
        for h in range(2):
            UT[h] = jnp.ones((crows, LANES), F32)
            row_parts(h)
        stage1(0)
        stage2(0)
        SV[c] = finish(0)
        send_wrap(1)
        send(SV.at[c], SV.at[c], v_send.at[0], v_recv.at[0], at(mc=1))
        send(SV.at[c], SV.at[c], v_send.at[1], v_recv.at[1], at(mr=1))
        send(SV.at[c], SV.at[c], v_send.at[2], v_recv.at[2], at(mr=1, mc=1))
        forward()
        arrived(SV.at[1 - c], v_recv.at[0])
        for h in range(2):
            expand(SV[h], COLS, h * half)
        arrived(EB.at[role, my_half], e_recv.at[0])
        exps(1, WO, g_own, inv_s, True)
        turn_student(WO, g_own)
        arrived(EB.at[1 - role, my_half], e_recv.at[2])
        arrived(WX, w_recv.at[0])
        exps(0, WX, 0, inv_t, False)
        arrived(UG, u_recv.at[0])
        scale_targets()
        arrived(AR2S, b_recv.at[0])
        total = AR2S[0]
        for m in range(1, nx * nyh):
            total = total + AR2S[m]
        R3V[c] = 1.0 / total

    send(R3V.at[c], R3V.at[c], r_send.at[0], r_recv.at[0], at(mc=1))

    def logit_grads(h):
        expand(R3V[h], COL3, h * half)

        def body(i, _):
            rows = pl.ds(pl.multiple_of(h * half + i * 16, 16), 16)
            t = AB[0, rows, :] * across(COL3[rows, :], PG)
            G[rows, :] = ((AB[1, rows, :] - t.astype(BF16).astype(F32)) * 10.0).astype(BF16)
            return 0

        lax.fori_loop(0, half // 16, body, 0)

    def embed_parts(h):
        rows = pl.ds(pl.multiple_of(h * half, half), half)

        def body(j, _):
            cols = pl.ds(pl.multiple_of(j * TILE, TILE), TILE)
            EGP[h, :, cols] = jnp.dot(G[rows, :], WT[:, cols], preferred_element_type=F32)
            return 0

        lax.fori_loop(0, D // TILE, body, 0)

    xrows = half // nx
    yrows = xrows // nyh
    owned = yrows // nz

    def x_rows(m):
        return pl.ds(pl.multiple_of((x ^ m) * xrows, xrows), xrows)

    logit_grads(c)
    arrived(R3V.at[1 - c], r_recv.at[0])
    logit_grads(1 - c)
    embed_parts(1 - c)
    for m in x_peers + [0]:
        send(EGP.at[1 - c, x_rows(m)], RC.at[x_rows(m)], c_send.at[m], c_recv.at[m], at(mc=1))
    embed_parts(c)
    for h in range(nyh):
        for m in x_peers + [0]:
            rows = pl.ds(pl.multiple_of((x ^ m) * xrows + h * yrows, yrows), yrows)
            if h == 0:
                arrived(RC.at[x_rows(m)], c_recv.at[m])
            EGP[c, rows, :] = EGP[c, rows, :] + RC[rows, :]
            if m:
                send(EGP.at[c, rows], RX.at[h, m - 1], x_send.at[h], x_recv.at[h], at(mx=m))

    my_q = 2 * c + role
    out_first = c * PC + role * PG

    def wg_tile(j, _):
        cols = pl.ds(pl.multiple_of(j * TILE, TILE), TILE)
        WGB[:, cols] = jnp.dot(ET[...], G[:, cols], preferred_element_type=F32).astype(BF16)
        dst = wg_out.at[0, 0, :, pl.ds(pl.multiple_of(out_first + j * TILE, TILE), TILE)]
        for m in (1, 3, 2):
            src = WGB.at[pl.ds(pl.multiple_of((my_q ^ m) * quarter, quarter), quarter), cols]
            send(src, dst, g_send.at[0], g_recv.at[0], at(mr=m % 2, mc=m // 2))
        return 0

    lax.fori_loop(0, PG // TILE, wg_tile, 0)
    mine = pltpu.make_async_copy(
        WGB.at[pl.ds(pl.multiple_of(my_q * quarter, quarter), quarter)],
        wg_out.at[0, 0, :, pl.ds(pl.multiple_of(out_first, PG), PG)], g_loc.at[0])
    mine.start()

    for h in range(nyh):
        rows = pl.ds(pl.multiple_of(x * xrows + h * yrows, yrows), yrows)
        arrived(RX.at[h], x_recv.at[h])
        total = EGP[c, rows, :]
        for m in range(nx - 1):
            total = total + RX[h, m]
        S1[h] = total.reshape(nz, owned, D)
        for m in z_peers:
            send(S1.at[h, z ^ m], RZ.at[h, m - 1], z_send.at[h], z_recv.at[h], at(mz=m))
    for h in range(nyh):
        part = S1[h, z]
        if nz > 1:
            arrived(RZ.at[h], z_recv.at[h])
            for m in range(nz - 1):
                part = part + RZ[h, m]
        for g in range(2):
            S2[g, h] = part[:, g * (D // 2):(g + 1) * (D // 2)]
    for m in range(1, 2 * nyh):
        send(S2.at[role ^ (m % 2), yh ^ (m // 2)], RY.at[m - 1], y_send.at[0], y_recv.at[0],
             at(mr=m % 2, my=m // 2))
    arrived(RY, y_recv.at[0])
    out = S2[role, yh]
    for m in range(2 * nyh - 1):
        out = out + RY[m]
    eg_out[...] = out

    arrived(EB.at[role, my_half], e_send.at[0])
    arrived(EB.at[role, my_half], e_send.at[1])
    arrived(EB.at[role, my_half], e_send.at[2])
    arrived(WX, w_send.at[0])
    arrived(R3V.at[c], r_send.at[0])

    def sent(it):
        if nz > 1:
            arrived(AR1.at[it], a1s.at[it])
        arrived(AR2.at[it], a2s.at[it])

    sent(0)

    @pl.when(teacher)
    def _():
        sent(1)
        sent(2)
        for it in range(3):
            for h in range(2):
                arrived(PCS.at[it, h], p_send.at[it, h])
        arrived(UG, u_send.at[0])
        arrived(AR2S, b_send.at[0])

    @pl.when(student)
    def _():
        for k in range(3):
            arrived(SV.at[0], v_send.at[k])

    for m in range(nx):
        arrived(RC.at[pl.ds(0, xrows)], c_send.at[m])
    for h in range(nyh):
        arrived(RX.at[h], x_send.at[h])
        if nz > 1:
            arrived(RZ.at[h], z_send.at[h])
    arrived(RY, y_send.at[0])
    three = wg_out.at[0, 0, :, pl.ds(0, 3 * PG)]
    arrived(three, g_recv.at[0])
    arrived(three, g_send.at[0])
    mine.wait()


def solution(mesh):
    chips = CHIPS[mesh.shape["proto"]]
    nx, nyh, nz = chips

    def per_device(emb, wgt):
        half, D = emb.shape[1:]
        B, PB = 2 * half, wgt.shape[2]
        PC, PG = PB // 2, PB // 4
        vrows, xrows = half // LANES, half // nx
        yrows = xrows // nyh
        owned = yrows // nz
        dma = lambda *shape: pltpu.SemaphoreType.DMA(shape)
        wg, eg = pl.pallas_call(
            functools.partial(kernel, chips),
            name="head_step",
            out_shape=(
                jax.ShapeDtypeStruct((1, 1, D // 4, PB), BF16),
                jax.ShapeDtypeStruct((owned, D // 2), F32),
            ),
            in_specs=[pl.BlockSpec(memory_space=pl.ANY)] * 2,
            out_specs=(pl.BlockSpec(memory_space=pl.ANY), pl.BlockSpec(memory_space=pltpu.VMEM)),
            scratch_shapes=[
                pltpu.VMEM((2, B, D), BF16),
                pltpu.VMEM((D, PB), BF16),
                pltpu.VMEM((D, PG), BF16),
                pltpu.VMEM((half, PB), F32),
                pltpu.VMEM((2, B, PG), F32),
                pltpu.VMEM((B, PG), BF16),
                pltpu.VMEM((D, B), BF16),
                pltpu.VMEM((PG, D), BF16),
                pltpu.VMEM((3, 2, PC // LANES, LANES), F32),
                pltpu.VMEM((3, 2, PC // LANES, LANES), F32),
                pltpu.VMEM((2, PC // LANES, LANES), F32),
                pltpu.VMEM((PG // LANES, LANES), F32),
                pltpu.VMEM((half, LANES), F32),
                pltpu.VMEM((half, LANES), F32),
                pltpu.VMEM((B, LANES), F32),
                pltpu.VMEM((B, LANES), F32),
                pltpu.VMEM((3, vrows, LANES), F32),
                pltpu.VMEM((3, vrows, LANES), F32),
                pltpu.VMEM((3, max(nz - 1, 1), vrows, LANES), F32),
                pltpu.VMEM((3, nx * nyh - 1, vrows, LANES), F32),
                pltpu.VMEM((nx * nyh, vrows, LANES), F32),
                pltpu.VMEM((3, vrows, LANES), F32),
                pltpu.VMEM((2, vrows, LANES), F32),
                pltpu.VMEM((2, vrows, LANES), F32),
                pltpu.VMEM((2, half, D), F32),
                pltpu.VMEM((half, D), F32),
                pltpu.VMEM((nyh, nx - 1, yrows, D), F32),
                pltpu.VMEM((nyh, nz, owned, D), F32),
                pltpu.VMEM((nyh, max(nz - 1, 1), owned, D), F32),
                pltpu.VMEM((2, nyh, owned, D // 2), F32),
                pltpu.VMEM((2 * nyh - 1, owned, D // 2), F32),
                pltpu.VMEM((D, PG), BF16),
                dma(1), dma(4), dma(3), dma(3), dma(1), dma(1), dma(3, 2), dma(3, 2),
                dma(3), dma(3), dma(3), dma(3), dma(1), dma(1),
                dma(1), dma(1), dma(3), dma(3), dma(1), dma(1), dma(nx), dma(nx), dma(nyh), dma(nyh),
                dma(nyh), dma(nyh), dma(1), dma(1), dma(1), dma(1), dma(1),
            ],
            compiler_params=pltpu.CompilerParams(
                collective_id=0, has_side_effects=True, vmem_limit_bytes=56 * 1024 * 1024),
            cost_estimate=pl.CostEstimate(
                flops=2 * B * D * PG * 6, bytes_accessed=2 * D * PB, transcendentals=4 * B * PG),
        )(emb, wgt)
        return wg, eg.astype(BF16)[None]

    return jax.shard_map(
        per_device,
        mesh=mesh,
        in_specs=(P("role", "crop", None), P("role", None, "proto")),
        out_specs=(P("crop", "role", None, "proto"), P("crop", "proto", "role")),
        check_vma=False,
    )
```

```python
import functools

import jax
import jax.numpy as jnp
from jax import lax
from jax.experimental import pallas as pl
from jax.experimental.pallas import tpu as pltpu
from jax.sharding import PartitionSpec as P

F32 = jnp.float32
BF16 = jnp.bfloat16
MESH = pl.DeviceIdType.MESH
LANES = 128
TILE = 256
CHIPS = {64: (4, 2, 8), 8: (2, 2, 2), 4: (2, 2, 1)}
BATCHES = (5, 6, 5)


def across(column, width):
    return jnp.concatenate([column] * (width // LANES), axis=1)


def far_first(n):
    return sorted(range(1, n), key=lambda m: -max(min(abs(a - (a ^ m)), n - abs(a - (a ^ m))) for a in range(n)))


def kernel(chips, emb, wgt, wg_out, eg_out,
           EB, WO, WX, KC, AB, G, ET, WT, PCS, PCR, UT, UG, RS, COLR, COLS, COL3,
           SRC1, SRC2, AR1, AR2, AR2S, SV, R3V, EGP, RC, RX, S1, RZ, S2, RY, WGB,
           loc, w_loc, e_send, e_recv, w_send, w_recv, p_send, p_recv, a1s, a1r, a2s, a2r, b_send, b_recv,
           u_send, u_recv, v_send, v_recv, r_send, r_recv, c_send, c_recv, x_send, x_recv,
           z_send, z_recv, y_send, y_recv, g_send, g_recv, g_loc):
    nx, nyh, nz = chips
    role, p, c = (lax.axis_index(a) for a in ("role", "proto", "crop"))
    x, yh, z = p // (nyh * nz), (p // nz) % nyh, p % nz
    teacher = role == 0
    student = role == 1
    half, D = emb.shape[1], emb.shape[2]
    B = 2 * half
    PB = wgt.shape[2]
    PC, PG = PB // 2, PB // 4
    vrows = half // LANES
    crows, grows = PC // LANES, PG // LANES
    quarter = D // 4

    def at(mr=0, mx=0, my=0, mz=0, mc=0):
        return {"role": role ^ mr, "proto": p ^ ((mx * nyh + my) * nz + mz), "crop": c ^ mc}

    def send(src, dst, s, r, to):
        pltpu.make_async_remote_copy(
            src_ref=src, dst_ref=dst, send_sem=s, recv_sem=r, device_id=to, device_id_type=MESH).start()

    def arrived(ref, sem):
        pltpu.make_async_copy(ref, ref, sem).wait()

    z_peers = far_first(nz)
    x_peers = far_first(nx)
    xy_peers = sorted(range(1, nx * nyh), key=lambda m: -((m // nyh in (1, 3)) + 2 * (m // nyh == 2) + 2 * (m % nyh)))

    barrier = pltpu.get_barrier_semaphore()
    greeted = [at(mz=m) for m in z_peers] + [at(mx=m // nyh, my=m % nyh) for m in xy_peers]
    greeted += [at(mr=1, mx=m // nyh, my=m % nyh) for m in range(nx * nyh)] + [at(mc=1), at(mr=1, mc=1)]
    for to in greeted:
        pl.semaphore_signal(barrier, inc=1, device_id=to, device_id_type=MESH)

    my_half = pl.ds(pl.multiple_of(c * half, half), half)
    own_e = pltpu.make_async_copy(emb.at[0], EB.at[role, my_half], loc.at[0])
    own_e.start()
    own_w = []
    for k in range(4):
        cols = pl.ds(k * PG, PG)
        own_w.append(pltpu.make_async_copy(wgt.at[0, :, cols], WO.at[:, cols], w_loc.at[k]))
        own_w[-1].start()

    inv_t, inv_s = 1.0 / 0.07, 1.0 / 0.1
    scale = jnp.where(teacher, inv_t, inv_s).astype(F32)

    own_e.wait()
    for k in range(4):
        own_w[k].wait()

        def own_tile(j, _, k=k):
            cols = pl.ds(pl.multiple_of(k * PG + j * TILE, TILE), TILE)
            s = jnp.dot(EB[role, my_half, :], WO[:, cols], preferred_element_type=F32)
            a = jnp.exp(s * scale)
            KC[:, cols] = a
            cs = jnp.sum(a, axis=0, keepdims=True)
            for l in range(TILE // LANES):
                PCS[0, k // 2, pl.ds((k % 2) * grows + j * (TILE // LANES) + l, 1), :] = cs[:, l * LANES:(l + 1) * LANES]
            return 0

        lax.fori_loop(0, PG // TILE, own_tile, 0)

    pl.semaphore_wait(barrier, len(greeted))

    g_own = pl.multiple_of(c * PC + role * PG, PG)
    g_away = pl.multiple_of(c * PC + (1 - role) * PG, PG)
    step_rows = D // sum(BATCHES)

    def send_columns(it, h):
        send(PCS.at[it, h], PCR.at[it, h], p_send.at[it, h], p_recv.at[it, h], at(mc=1))

    def send_core():
        send(emb.at[0], EB.at[role, my_half], e_send.at[0], e_recv.at[0], at(mc=1))

    def send_wrap(h):
        rows = pl.ds(h * (half // 2), half // 2)
        there = pl.ds(pl.multiple_of(c * half + h * (half // 2), half // 2), half // 2)
        send(emb.at[0, rows], EB.at[role, there], e_send.at[1], e_recv.at[1], at(mr=1, my=1))

    def send_weights(k):
        for q in range(sum(BATCHES[:k]), sum(BATCHES[:k + 1])):
            rows = pl.ds(q * step_rows, step_rows)
            send(wgt.at[0, rows, pl.ds(g_away, PG)], WX.at[rows, :], w_send.at[0], w_recv.at[0], at(mr=1))

    def expand(vec, ref, first=0):
        for i in range(vrows):
            rows = pl.ds(pl.multiple_of(first + i * LANES, LANES), LANES)
            ref[rows, :] = jnp.broadcast_to(vec[i:i + 1, :], (LANES, LANES)).T

    def column_parts(it, h):
        def body(i, acc):
            for k in range(4):
                rows = pl.ds(pl.multiple_of(i * 32 + k * 8, 8), 8)
                acc = acc + KC[rows, h * PC:(h + 1) * PC] * across(COLR[rows, :], PC)
            return acc

        acc = lax.fori_loop(0, half // 32, body, jnp.zeros((8, PC), F32))
        cs = jnp.sum(acc, axis=0, keepdims=True)
        for l in range(crows):
            PCS[it, h, l:l + 1, :] = cs[:, l * LANES:(l + 1) * LANES]
        send_columns(it, h)

    def column_scales(it, h):
        arrived(PCR.at[it, h], p_recv.at[it, h])
        UT[h] = 1.0 / (PCS[it, h] + PCR[it, h])

    def row_parts(h):
        ub = jnp.concatenate(
            [jnp.broadcast_to(UT[h, l:l + 1, :], (8, LANES)) for l in range(crows)], axis=1)

        def body(i, _):
            for k in range(4):
                rows = pl.ds(pl.multiple_of(i * 32 + k * 8, 8), 8)
                m = KC[rows, h * PC:(h + 1) * PC] * ub
                parts = [m[:, l * LANES:(l + 1) * LANES] for l in range(crows)]
                while len(parts) > 1:
                    parts = [a + b for a, b in zip(parts[::2], parts[1::2])]
                RS[rows, :] = parts[0] if h == 0 else RS[rows, :] + parts[0]
            return 0

        lax.fori_loop(0, half // 32, body, 0)

    def stage1(it):
        for i in range(vrows):
            SRC1[it, i:i + 1, :] = jnp.sum(RS[i * LANES:(i + 1) * LANES, :].T, axis=0, keepdims=True)
        for m in z_peers:
            send(SRC1.at[it], AR1.at[it, m - 1], a1s.at[it], a1r.at[it], at(mz=m))

    def stage2(it):
        total = SRC1[it]
        if nz > 1:
            arrived(AR1.at[it], a1r.at[it])
            for m in range(nz - 1):
                total = total + AR1[it, m]
        SRC2[it] = total
        for m in xy_peers:
            send(SRC2.at[it], AR2.at[it, m - 1], a2s.at[it], a2r.at[it], at(mx=m // nyh, my=m % nyh))
        if it == 2:
            for m in range(nx * nyh):
                send(SRC2.at[it], AR2S.at[m], b_send.at[0], b_recv.at[0], at(mr=1, mx=m // nyh, my=m % nyh))

    def finish(it):
        arrived(AR2.at[it], a2r.at[it])
        total = SRC2[it]
        for m in range(nx * nyh - 1):
            total = total + AR2[it, m]
        return 1.0 / total

    def forward():
        arrived(EB.at[1 - role, my_half], e_recv.at[1])
        send(EB.at[1 - role, my_half], EB.at[1 - role, my_half], e_send.at[2], e_recv.at[2], at(mc=1))

    def exps(which, weights, first, inv, scaled):
        def tile(j, _):
            cols = pl.ds(pl.multiple_of(j * TILE, TILE), TILE)
            w_cols = pl.ds(pl.multiple_of(first + j * TILE, TILE), TILE)
            s = jnp.dot(EB[which], weights[:, w_cols], preferred_element_type=F32)
            a = jnp.exp(s * inv)
            AB[which, :, cols] = a * across(COLS[...], TILE) if scaled else a
            return 0

        lax.fori_loop(0, PG // TILE, tile, 0)

    def scale_targets():
        ub = jnp.concatenate(
            [jnp.broadcast_to(UG[l:l + 1, :], (8, LANES)) for l in range(grows)], axis=1)

        def body(i, _):
            for k in range(4):
                rows = pl.ds(pl.multiple_of(i * 32 + k * 8, 8), 8)
                AB[0, rows, :] = AB[0, rows, :] * ub
            return 0

        lax.fori_loop(0, B // 32, body, 0)

    def turn_student(weights, first):
        for i in range(B // TILE):
            ET[:, i * TILE:(i + 1) * TILE] = EB[1, i * TILE:(i + 1) * TILE, :].T

        def body(i, _):
            rows = pl.ds(pl.multiple_of(i * TILE, TILE), TILE)
            WT[rows, :] = weights[:, pl.ds(pl.multiple_of(first + i * TILE, TILE), TILE)].T
            return 0

        lax.fori_loop(0, PG // TILE, body, 0)

    @pl.when(teacher)
    def _():
        for h in range(2):
            send_columns(0, h)
        send_core()
        send_wrap(0)
        send_weights(0)
        for h in range(2):
            column_scales(0, h)
            row_parts(h)
        stage1(0)
        arrived(EB.at[role, my_half], e_recv.at[0])
        exps(0, WO, g_own, inv_t, False)
        stage2(0)
        r = finish(0)
        for it in (1, 2):
            expand(r, COLR)
            send_weights(it)
            if it == 1:
                send_wrap(1)
            for h in range(2):
                column_parts(it, h)
            for h in range(2):
                column_scales(it, h)
                row_parts(h)
            stage1(it)
            if it == 2:
                UG[...] = UT[c, 0:grows, :]
                send(UT.at[c, pl.ds(grows, grows)], UG, u_send.at[0], u_recv.at[0], at(mr=1))
                scale_targets()
                arrived(EB.at[1 - role, my_half], e_recv.at[2])
                arrived(WX, w_recv.at[0])
                turn_student(WX, 0)
            stage2(it)
            if it == 1:
                forward()
            else:
                arrived(SV.at[c], v_recv.at[1])
                arrived(SV.at[1 - c], v_recv.at[2])
                for h in range(2):
                    expand(SV[h], COLS, h * half)
                exps(1, WX, 0, inv_s, True)
            r = finish(it)
        R3V[c] = r

    @pl.when(student)
    def _():
        send_core()
        send_wrap(0)
        send_wrap(1)
        send_weights(0)
        for h in range(2):
            UT[h] = jnp.ones((crows, LANES), F32)
            row_parts(h)
        stage1(0)
        stage2(0)
        SV[c] = finish(0)
        send(SV.at[c], SV.at[c], v_send.at[0], v_recv.at[0], at(mc=1))
        send(SV.at[c], SV.at[c], v_send.at[1], v_recv.at[1], at(mr=1))
        send(SV.at[c], SV.at[c], v_send.at[2], v_recv.at[2], at(mr=1, mc=1))
        for k in range(1, len(BATCHES)):
            send_weights(k)
        forward()
        arrived(SV.at[1 - c], v_recv.at[0])
        for h in range(2):
            expand(SV[h], COLS, h * half)
        arrived(EB.at[role, my_half], e_recv.at[0])
        exps(1, WO, g_own, inv_s, True)
        turn_student(WO, g_own)
        arrived(EB.at[1 - role, my_half], e_recv.at[2])
        arrived(WX, w_recv.at[0])
        exps(0, WX, 0, inv_t, False)
        arrived(UG, u_recv.at[0])
        scale_targets()
        arrived(AR2S, b_recv.at[0])
        total = AR2S[0]
        for m in range(1, nx * nyh):
            total = total + AR2S[m]
        R3V[c] = 1.0 / total

    send(R3V.at[c], R3V.at[c], r_send.at[0], r_recv.at[0], at(mc=1))

    def logit_grads(h):
        expand(R3V[h], COL3, h * half)

        def body(i, _):
            rows = pl.ds(pl.multiple_of(h * half + i * 16, 16), 16)
            t = AB[0, rows, :] * across(COL3[rows, :], PG)
            G[rows, :] = ((AB[1, rows, :] - t.astype(BF16).astype(F32)) * 10.0).astype(BF16)
            return 0

        lax.fori_loop(0, half // 16, body, 0)

    def embed_parts(h):
        rows = pl.ds(pl.multiple_of(h * half, half), half)

        def body(j, _):
            cols = pl.ds(pl.multiple_of(j * TILE, TILE), TILE)
            EGP[h, :, cols] = jnp.dot(G[rows, :], WT[:, cols], preferred_element_type=F32)
            return 0

        lax.fori_loop(0, D // TILE, body, 0)

    xrows = half // nx
    yrows = xrows // nyh
    owned = yrows // nz

    def x_rows(m):
        return pl.ds(pl.multiple_of((x ^ m) * xrows, xrows), xrows)

    logit_grads(c)
    arrived(R3V.at[1 - c], r_recv.at[0])
    logit_grads(1 - c)
    embed_parts(1 - c)
    for m in x_peers + [0]:
        send(EGP.at[1 - c, x_rows(m)], RC.at[x_rows(m)], c_send.at[m], c_recv.at[m], at(mc=1))
    embed_parts(c)
    for h in range(nyh):
        for m in x_peers + [0]:
            rows = pl.ds(pl.multiple_of((x ^ m) * xrows + h * yrows, yrows), yrows)
            if h == 0:
                arrived(RC.at[x_rows(m)], c_recv.at[m])
            EGP[c, rows, :] = EGP[c, rows, :] + RC[rows, :]
            if m:
                send(EGP.at[c, rows], RX.at[h, m - 1], x_send.at[h], x_recv.at[h], at(mx=m))

    my_q = 2 * c + role
    out_first = c * PC + role * PG

    def wg_tile(j, _):
        cols = pl.ds(pl.multiple_of(j * TILE, TILE), TILE)
        WGB[:, cols] = jnp.dot(ET[...], G[:, cols], preferred_element_type=F32).astype(BF16)
        dst = wg_out.at[0, 0, :, pl.ds(pl.multiple_of(out_first + j * TILE, TILE), TILE)]
        for m in (1, 3, 2):
            src = WGB.at[pl.ds(pl.multiple_of((my_q ^ m) * quarter, quarter), quarter), cols]
            send(src, dst, g_send.at[0], g_recv.at[0], at(mr=m % 2, mc=m // 2))
        return 0

    lax.fori_loop(0, PG // TILE, wg_tile, 0)
    mine = pltpu.make_async_copy(
        WGB.at[pl.ds(pl.multiple_of(my_q * quarter, quarter), quarter)],
        wg_out.at[0, 0, :, pl.ds(pl.multiple_of(out_first, PG), PG)], g_loc.at[0])
    mine.start()

    for h in range(nyh):
        rows = pl.ds(pl.multiple_of(x * xrows + h * yrows, yrows), yrows)
        arrived(RX.at[h], x_recv.at[h])
        total = EGP[c, rows, :]
        for m in range(nx - 1):
            total = total + RX[h, m]
        S1[h] = total.reshape(nz, owned, D)
        for m in z_peers:
            send(S1.at[h, z ^ m], RZ.at[h, m - 1], z_send.at[h], z_recv.at[h], at(mz=m))
    for h in range(nyh):
        part = S1[h, z]
        if nz > 1:
            arrived(RZ.at[h], z_recv.at[h])
            for m in range(nz - 1):
                part = part + RZ[h, m]
        for g in range(2):
            S2[g, h] = part[:, g * (D // 2):(g + 1) * (D // 2)]
    for m in range(1, 2 * nyh):
        send(S2.at[role ^ (m % 2), yh ^ (m // 2)], RY.at[m - 1], y_send.at[0], y_recv.at[0],
             at(mr=m % 2, my=m // 2))
    arrived(RY, y_recv.at[0])
    out = S2[role, yh]
    for m in range(2 * nyh - 1):
        out = out + RY[m]
    eg_out[...] = out

    arrived(EB.at[role, my_half], e_send.at[0])
    arrived(EB.at[role, my_half], e_send.at[1])
    arrived(EB.at[role, my_half], e_send.at[2])
    arrived(WX, w_send.at[0])
    arrived(R3V.at[c], r_send.at[0])

    def sent(it):
        if nz > 1:
            arrived(AR1.at[it], a1s.at[it])
        arrived(AR2.at[it], a2s.at[it])

    sent(0)

    @pl.when(teacher)
    def _():
        sent(1)
        sent(2)
        for it in range(3):
            for h in range(2):
                arrived(PCS.at[it, h], p_send.at[it, h])
        arrived(UG, u_send.at[0])
        arrived(AR2S, b_send.at[0])

    @pl.when(student)
    def _():
        for k in range(3):
            arrived(SV.at[0], v_send.at[k])

    for m in range(nx):
        arrived(RC.at[pl.ds(0, xrows)], c_send.at[m])
    for h in range(nyh):
        arrived(RX.at[h], x_send.at[h])
        if nz > 1:
            arrived(RZ.at[h], z_send.at[h])
    arrived(RY, y_send.at[0])
    three = wg_out.at[0, 0, :, pl.ds(0, 3 * PG)]
    arrived(three, g_recv.at[0])
    arrived(three, g_send.at[0])
    mine.wait()


def solution(mesh):
    chips = CHIPS[mesh.shape["proto"]]
    nx, nyh, nz = chips

    def per_device(emb, wgt):
        half, D = emb.shape[1:]
        B, PB = 2 * half, wgt.shape[2]
        PC, PG = PB // 2, PB // 4
        vrows, xrows = half // LANES, half // nx
        yrows = xrows // nyh
        owned = yrows // nz
        dma = lambda *shape: pltpu.SemaphoreType.DMA(shape)
        wg, eg = pl.pallas_call(
            functools.partial(kernel, chips),
            name="head_step",
            out_shape=(
                jax.ShapeDtypeStruct((1, 1, D // 4, PB), BF16),
                jax.ShapeDtypeStruct((owned, D // 2), F32),
            ),
            in_specs=[pl.BlockSpec(memory_space=pl.ANY)] * 2,
            out_specs=(pl.BlockSpec(memory_space=pl.ANY), pl.BlockSpec(memory_space=pltpu.VMEM)),
            scratch_shapes=[
                pltpu.VMEM((2, B, D), BF16),
                pltpu.VMEM((D, PB), BF16),
                pltpu.VMEM((D, PG), BF16),
                pltpu.VMEM((half, PB), F32),
                pltpu.VMEM((2, B, PG), F32),
                pltpu.VMEM((B, PG), BF16),
                pltpu.VMEM((D, B), BF16),
                pltpu.VMEM((PG, D), BF16),
                pltpu.VMEM((3, 2, PC // LANES, LANES), F32),
                pltpu.VMEM((3, 2, PC // LANES, LANES), F32),
                pltpu.VMEM((2, PC // LANES, LANES), F32),
                pltpu.VMEM((PG // LANES, LANES), F32),
                pltpu.VMEM((half, LANES), F32),
                pltpu.VMEM((half, LANES), F32),
                pltpu.VMEM((B, LANES), F32),
                pltpu.VMEM((B, LANES), F32),
                pltpu.VMEM((3, vrows, LANES), F32),
                pltpu.VMEM((3, vrows, LANES), F32),
                pltpu.VMEM((3, max(nz - 1, 1), vrows, LANES), F32),
                pltpu.VMEM((3, nx * nyh - 1, vrows, LANES), F32),
                pltpu.VMEM((nx * nyh, vrows, LANES), F32),
                pltpu.VMEM((2, vrows, LANES), F32),
                pltpu.VMEM((2, vrows, LANES), F32),
                pltpu.VMEM((2, half, D), F32),
                pltpu.VMEM((half, D), F32),
                pltpu.VMEM((nyh, nx - 1, yrows, D), F32),
                pltpu.VMEM((nyh, nz, owned, D), F32),
                pltpu.VMEM((nyh, max(nz - 1, 1), owned, D), F32),
                pltpu.VMEM((2, nyh, owned, D // 2), F32),
                pltpu.VMEM((2 * nyh - 1, owned, D // 2), F32),
                pltpu.VMEM((D, PG), BF16),
                dma(1), dma(4), dma(3), dma(3), dma(1), dma(1), dma(3, 2), dma(3, 2),
                dma(3), dma(3), dma(3), dma(3), dma(1), dma(1),
                dma(1), dma(1), dma(3), dma(3), dma(1), dma(1), dma(nx), dma(nx), dma(nyh), dma(nyh),
                dma(nyh), dma(nyh), dma(1), dma(1), dma(1), dma(1), dma(1),
            ],
            compiler_params=pltpu.CompilerParams(
                collective_id=0, has_side_effects=True, vmem_limit_bytes=56 * 1024 * 1024),
            cost_estimate=pl.CostEstimate(
                flops=2 * B * D * PG * 6, bytes_accessed=2 * D * PB, transcendentals=4 * B * PG),
        )(emb, wgt)
        return wg, eg.astype(BF16)[None]

    return jax.shard_map(
        per_device,
        mesh=mesh,
        in_specs=(P("role", "crop", None), P("role", None, "proto")),
        out_specs=(P("crop", "role", None, "proto"), P("crop", "proto", "role")),
        check_vma=False,
    )
```

```python
import functools

import jax
import jax.numpy as jnp
from jax import lax
from jax.experimental import pallas as pl
from jax.experimental.pallas import tpu as pltpu
from jax.sharding import PartitionSpec as P

F32 = jnp.float32
BF16 = jnp.bfloat16
MESH = pl.DeviceIdType.MESH
LANES = 128
TILE = 256
CHIPS = {64: (4, 2, 8), 8: (2, 2, 2), 4: (2, 2, 1)}
BATCHES = (5, 6, 5)


def across(column, width):
    return jnp.concatenate([column] * (width // LANES), axis=1)


def far_first(n):
    return sorted(range(1, n), key=lambda m: -max(min(abs(a - (a ^ m)), n - abs(a - (a ^ m))) for a in range(n)))


def kernel(chips, emb, wgt, wg_out, eg_out,
           EB, WO, WX, KC, AB, G, ET, WT, PCS, PCR, UT, UG, RS, COLR, COLS, COL3,
           SRC1, ALL, SRC2, AR1, AR2, AR2S, SV, R3V, EGP, RC, RX, S1, RZ, WGB,
           loc, w_loc, e_send, e_recv, w_send, w_recv, p_send, p_recv, a1s, a1r, a2s, a2r, b_send, b_recv,
           u_send, u_recv, v_send, v_recv, r_send, r_recv, c_send, c_recv, x_send, x_recv,
           z_send, z_recv, g_send, g_recv, g_loc):
    nx, nyh, nz = chips
    role, p, c = (lax.axis_index(a) for a in ("role", "proto", "crop"))
    x, yh, z = p // (nyh * nz), (p // nz) % nyh, p % nz
    teacher = role == 0
    student = role == 1
    half, D = emb.shape[1], emb.shape[2]
    B = 2 * half
    PB = wgt.shape[2]
    PC, PG = PB // 2, PB // 4
    vrows = half // LANES
    crows, grows = PC // LANES, PG // LANES
    quarter = D // 4

    def at(mr=0, mx=0, my=0, mz=0, mc=0):
        return {"role": role ^ mr, "proto": p ^ ((mx * nyh + my) * nz + mz), "crop": c ^ mc}

    def send(src, dst, s, r, to):
        pltpu.make_async_remote_copy(
            src_ref=src, dst_ref=dst, send_sem=s, recv_sem=r, device_id=to, device_id_type=MESH).start()

    def arrived(ref, sem):
        pltpu.make_async_copy(ref, ref, sem).wait()

    z_peers = far_first(nz)
    x_peers = far_first(nx)
    def hops(m):
        far = 0
        for n, k in ((nx, m // (nyh * nz)), (nz, m % nz)):
            far += max(min(abs(a - (a ^ k)), n - abs(a - (a ^ k))) for a in range(n))
        return far + 2 * ((m // nz) % nyh)

    all_peers = sorted(range(1, nx * nyh * nz), key=lambda m: -hops(m))
    xy_peers = sorted(range(1, nx * nyh), key=lambda m: -((m // nyh in (1, 3)) + 2 * (m // nyh == 2) + 2 * (m % nyh)))

    barrier = pltpu.get_barrier_semaphore()
    greeted = [at(mz=m) for m in z_peers] + [at(mx=m // nyh, my=m % nyh) for m in xy_peers]
    greeted += [at(mr=1, mx=m // nyh, my=m % nyh) for m in range(nx * nyh)] + [at(mc=1), at(mr=1, mc=1)]
    for to in greeted:
        pl.semaphore_signal(barrier, inc=1, device_id=to, device_id_type=MESH)

    my_half = pl.ds(pl.multiple_of(c * half, half), half)
    own_e = pltpu.make_async_copy(emb.at[0], EB.at[role, my_half], loc.at[0])
    own_e.start()
    own_w = []
    for k in range(4):
        cols = pl.ds(k * PG, PG)
        own_w.append(pltpu.make_async_copy(wgt.at[0, :, cols], WO.at[:, cols], w_loc.at[k]))
        own_w[-1].start()

    inv_t, inv_s = 1.0 / 0.07, 1.0 / 0.1
    scale = jnp.where(teacher, inv_t, inv_s).astype(F32)

    own_e.wait()
    for k in range(4):
        own_w[k].wait()

        def own_tile(j, _, k=k):
            cols = pl.ds(pl.multiple_of(k * PG + j * TILE, TILE), TILE)
            s = jnp.dot(EB[role, my_half, :], WO[:, cols], preferred_element_type=F32)
            a = jnp.exp(s * scale)
            KC[:, cols] = a
            cs = jnp.sum(a, axis=0, keepdims=True)
            for l in range(TILE // LANES):
                PCS[0, k // 2, pl.ds((k % 2) * grows + j * (TILE // LANES) + l, 1), :] = cs[:, l * LANES:(l + 1) * LANES]
            return 0

        lax.fori_loop(0, PG // TILE, own_tile, 0)

    pl.semaphore_wait(barrier, len(greeted))

    g_own = pl.multiple_of(c * PC + role * PG, PG)
    g_away = pl.multiple_of(c * PC + (1 - role) * PG, PG)
    step_rows = D // sum(BATCHES)

    def send_columns(it, h):
        send(PCS.at[it, h], PCR.at[it, h], p_send.at[it, h], p_recv.at[it, h], at(mc=1))

    def send_core():
        send(emb.at[0], EB.at[role, my_half], e_send.at[0], e_recv.at[0], at(mc=1))

    def send_wrap(h):
        rows = pl.ds(h * (half // 2), half // 2)
        there = pl.ds(pl.multiple_of(c * half + h * (half // 2), half // 2), half // 2)
        send(emb.at[0, rows], EB.at[role, there], e_send.at[1], e_recv.at[1], at(mr=1, my=1))

    def send_weights(k):
        for q in range(sum(BATCHES[:k]), sum(BATCHES[:k + 1])):
            rows = pl.ds(q * step_rows, step_rows)
            send(wgt.at[0, rows, pl.ds(g_away, PG)], WX.at[rows, :], w_send.at[0], w_recv.at[0], at(mr=1))

    def expand(vec, ref, first=0):
        for i in range(vrows):
            rows = pl.ds(pl.multiple_of(first + i * LANES, LANES), LANES)
            ref[rows, :] = jnp.broadcast_to(vec[i:i + 1, :], (LANES, LANES)).T

    def column_parts(it, h):
        def body(i, acc):
            for k in range(4):
                rows = pl.ds(pl.multiple_of(i * 32 + k * 8, 8), 8)
                acc = acc + KC[rows, h * PC:(h + 1) * PC] * across(COLR[rows, :], PC)
            return acc

        acc = lax.fori_loop(0, half // 32, body, jnp.zeros((8, PC), F32))
        cs = jnp.sum(acc, axis=0, keepdims=True)
        for l in range(crows):
            PCS[it, h, l:l + 1, :] = cs[:, l * LANES:(l + 1) * LANES]
        send_columns(it, h)

    def column_scales(it, h):
        arrived(PCR.at[it, h], p_recv.at[it, h])
        UT[h] = 1.0 / (PCS[it, h] + PCR[it, h])

    def row_parts(h):
        ub = jnp.concatenate(
            [jnp.broadcast_to(UT[h, l:l + 1, :], (8, LANES)) for l in range(crows)], axis=1)

        def body(i, _):
            for k in range(4):
                rows = pl.ds(pl.multiple_of(i * 32 + k * 8, 8), 8)
                m = KC[rows, h * PC:(h + 1) * PC] * ub
                parts = [m[:, l * LANES:(l + 1) * LANES] for l in range(crows)]
                while len(parts) > 1:
                    parts = [a + b for a, b in zip(parts[::2], parts[1::2])]
                RS[rows, :] = parts[0] if h == 0 else RS[rows, :] + parts[0]
            return 0

        lax.fori_loop(0, half // 32, body, 0)

    def stage1(it):
        for i in range(vrows):
            SRC1[it, i:i + 1, :] = jnp.sum(RS[i * LANES:(i + 1) * LANES, :].T, axis=0, keepdims=True)
        for m in all_peers if it == 1 else z_peers:
            send(SRC1.at[it], ALL.at[m - 1] if it == 1 else AR1.at[it, m - 1], a1s.at[it], a1r.at[it], at(mz=m))

    def stage2(it):
        total = SRC1[it]
        if nz > 1:
            arrived(AR1.at[it], a1r.at[it])
            for m in range(nz - 1):
                total = total + AR1[it, m]
        SRC2[it] = total
        for m in xy_peers:
            send(SRC2.at[it], AR2.at[it, m - 1], a2s.at[it], a2r.at[it], at(mx=m // nyh, my=m % nyh))
        if it == 2:
            for m in range(nx * nyh):
                send(SRC2.at[it], AR2S.at[m], b_send.at[0], b_recv.at[0], at(mr=1, mx=m // nyh, my=m % nyh))

    def finish(it):
        if it == 1:
            arrived(ALL, a1r.at[it])
            parts = [SRC1[it]] + [ALL[m] for m in range(nx * nyh * nz - 1)]
        else:
            arrived(AR2.at[it], a2r.at[it])
            parts = [SRC2[it]] + [AR2[it, m] for m in range(nx * nyh - 1)]
        while len(parts) > 1:
            parts = [a + b for a, b in zip(parts[::2], parts[1::2])]
        return 1.0 / parts[0]

    def forward():
        arrived(EB.at[1 - role, my_half], e_recv.at[1])
        send(EB.at[1 - role, my_half], EB.at[1 - role, my_half], e_send.at[2], e_recv.at[2], at(mc=1))

    def exps(which, weights, first, inv, scaled):
        def tile(j, _):
            cols = pl.ds(pl.multiple_of(j * TILE, TILE), TILE)
            w_cols = pl.ds(pl.multiple_of(first + j * TILE, TILE), TILE)
            s = jnp.dot(EB[which], weights[:, w_cols], preferred_element_type=F32)
            a = jnp.exp(s * inv)
            AB[which, :, cols] = a * across(COLS[...], TILE) if scaled else a
            return 0

        lax.fori_loop(0, PG // TILE, tile, 0)

    def scale_targets():
        ub = jnp.concatenate(
            [jnp.broadcast_to(UG[l:l + 1, :], (8, LANES)) for l in range(grows)], axis=1)

        def body(i, _):
            for k in range(4):
                rows = pl.ds(pl.multiple_of(i * 32 + k * 8, 8), 8)
                AB[0, rows, :] = AB[0, rows, :] * ub
            return 0

        lax.fori_loop(0, B // 32, body, 0)

    def turn_student(weights, first):
        for i in range(B // TILE):
            ET[:, i * TILE:(i + 1) * TILE] = EB[1, i * TILE:(i + 1) * TILE, :].T

        def body(i, _):
            rows = pl.ds(pl.multiple_of(i * TILE, TILE), TILE)
            WT[rows, :] = weights[:, pl.ds(pl.multiple_of(first + i * TILE, TILE), TILE)].T
            return 0

        lax.fori_loop(0, PG // TILE, body, 0)

    @pl.when(teacher)
    def _():
        for h in range(2):
            send_columns(0, h)
        send_core()
        send_wrap(0)
        send_weights(0)
        for h in range(2):
            column_scales(0, h)
            row_parts(h)
        stage1(0)
        arrived(EB.at[role, my_half], e_recv.at[0])
        exps(0, WO, g_own, inv_t, False)
        stage2(0)
        r = finish(0)
        for it in (1, 2):
            expand(r, COLR)
            send_weights(it)
            if it == 1:
                send_wrap(1)
            for h in range(2):
                column_parts(it, h)
            for h in range(2):
                column_scales(it, h)
                row_parts(h)
            stage1(it)
            if it == 2:
                UG[...] = UT[c, 0:grows, :]
                send(UT.at[c, pl.ds(grows, grows)], UG, u_send.at[0], u_recv.at[0], at(mr=1))
                scale_targets()
                arrived(EB.at[1 - role, my_half], e_recv.at[2])
                arrived(WX, w_recv.at[0])
                turn_student(WX, 0)
            if it == 1:
                forward()
            else:
                stage2(it)
                arrived(SV.at[c], v_recv.at[1])
                arrived(SV.at[1 - c], v_recv.at[2])
                for h in range(2):
                    expand(SV[h], COLS, h * half)
                exps(1, WX, 0, inv_s, True)
            r = finish(it)
        R3V[c] = r

    @pl.when(student)
    def _():
        send_core()
        send_wrap(0)
        send_wrap(1)
        send_weights(0)
        for h in range(2):
            UT[h] = jnp.ones((crows, LANES), F32)
            row_parts(h)
        stage1(0)
        stage2(0)
        SV[c] = finish(0)
        send(SV.at[c], SV.at[c], v_send.at[0], v_recv.at[0], at(mc=1))
        send(SV.at[c], SV.at[c], v_send.at[1], v_recv.at[1], at(mr=1))
        send(SV.at[c], SV.at[c], v_send.at[2], v_recv.at[2], at(mr=1, mc=1))
        for k in range(1, len(BATCHES)):
            send_weights(k)
        forward()
        arrived(SV.at[1 - c], v_recv.at[0])
        for h in range(2):
            expand(SV[h], COLS, h * half)
        arrived(EB.at[role, my_half], e_recv.at[0])
        exps(1, WO, g_own, inv_s, True)
        turn_student(WO, g_own)
        arrived(EB.at[1 - role, my_half], e_recv.at[2])
        arrived(WX, w_recv.at[0])
        exps(0, WX, 0, inv_t, False)
        arrived(UG, u_recv.at[0])
        scale_targets()
        arrived(AR2S, b_recv.at[0])
        total = AR2S[0]
        for m in range(1, nx * nyh):
            total = total + AR2S[m]
        R3V[c] = 1.0 / total

    send(R3V.at[c], R3V.at[c], r_send.at[0], r_recv.at[0], at(mc=1))

    xrows = half // nx
    yrows = xrows // nyh
    owned = yrows // nz
    side = half // 2
    blocks = nx // 2

    def side_rows(h, far):
        return pl.multiple_of(h * half + ((x // blocks) ^ far) * side, side)

    def logit_grads(h, far):
        def body(i, _):
            rows = pl.ds(pl.multiple_of(side_rows(h, far) + i * 16, 16), 16)
            t = AB[0, rows, :] * across(COL3[rows, :], PG)
            G[rows, :] = ((AB[1, rows, :] - t.astype(BF16).astype(F32)) * 10.0).astype(BF16)
            return 0

        lax.fori_loop(0, side // 16, body, 0)

    def embed_parts(h, far):
        rows = pl.ds(side_rows(h, far), side)
        local = pl.ds(pl.multiple_of(((x // blocks) ^ far) * side, side), side)

        def body(j, _):
            cols = pl.ds(pl.multiple_of(j * TILE, TILE), TILE)
            EGP[h, local, cols] = jnp.dot(G[rows, :], WT[:, cols], preferred_element_type=F32)
            return 0

        lax.fori_loop(0, D // TILE, body, 0)

    def x_rows(m):
        return pl.ds(pl.multiple_of((x ^ m) * xrows, xrows), xrows)

    far_side = list(range(blocks, nx))
    near_side = list(range(blocks - 1, -1, -1))

    def send_core_parts(masks):
        for m in masks:
            send(EGP.at[1 - c, x_rows(m)], RC.at[x_rows(m)], c_send.at[m], c_recv.at[m], at(mc=1))

    def send_x_parts(h, masks):
        for m in masks:
            rows = pl.ds(pl.multiple_of((x ^ m) * xrows + h * yrows, yrows), yrows)
            if h == 0:
                arrived(RC.at[x_rows(m)], c_recv.at[m])
            EGP[c, rows, :] = EGP[c, rows, :] + RC[rows, :]
            if m:
                send(EGP.at[c, rows], RX.at[h, m - 1], x_send.at[h], x_recv.at[h], at(mx=m))

    expand(R3V[c], COL3, c * half)
    logit_grads(c, 1)
    arrived(R3V.at[1 - c], r_recv.at[0])
    expand(R3V[1 - c], COL3, (1 - c) * half)
    logit_grads(1 - c, 1)
    embed_parts(1 - c, 1)
    send_core_parts(far_side)
    embed_parts(c, 1)
    logit_grads(1 - c, 0)
    embed_parts(1 - c, 0)
    send_core_parts(near_side)
    send_x_parts(0, far_side)
    logit_grads(c, 0)
    embed_parts(c, 0)
    send_x_parts(0, near_side)
    for h in range(1, nyh):
        send_x_parts(h, far_side + near_side)

    my_q = 2 * c + role
    out_first = c * PC + role * PG

    def wg_tile(j, _):
        cols = pl.ds(pl.multiple_of(j * TILE, TILE), TILE)
        WGB[:, cols] = jnp.dot(ET[...], G[:, cols], preferred_element_type=F32).astype(BF16)
        dst = wg_out.at[0, 0, :, pl.ds(pl.multiple_of(out_first + j * TILE, TILE), TILE)]
        for m in (1, 3, 2):
            src = WGB.at[pl.ds(pl.multiple_of((my_q ^ m) * quarter, quarter), quarter), cols]
            send(src, dst, g_send.at[0], g_recv.at[0], at(mr=m % 2, mc=m // 2))
        return 0

    lax.fori_loop(0, PG // TILE, wg_tile, 0)
    mine = pltpu.make_async_copy(
        WGB.at[pl.ds(pl.multiple_of(my_q * quarter, quarter), quarter)],
        wg_out.at[0, 0, :, pl.ds(pl.multiple_of(out_first, PG), PG)], g_loc.at[0])
    mine.start()

    for h in range(nyh):
        rows = pl.ds(pl.multiple_of(x * xrows + h * yrows, yrows), yrows)
        arrived(RX.at[h], x_recv.at[h])
        total = EGP[c, rows, :]
        for m in range(nx - 1):
            total = total + RX[h, m]
        S1[h] = total.reshape(nz, owned, D)
        my = yh ^ h
        for mz in z_peers + [0]:
            for mr in (1, 0):
                src = S1.at[h, z ^ mz, :, pl.ds(pl.multiple_of((role ^ mr) * (D // 2), D // 2), D // 2)]
                place = RZ.at[(my * 2 + mr) * nz + mz]

                def give(src=src, place=place, mr=mr, mz=mz):
                    send(src, place, z_send.at[0], z_recv.at[0], at(mr=mr, my=my, mz=mz))

                if mr or mz:
                    give()
                else:
                    pl.when(my != 0)(give)
    last = RZ.at[pl.ds(1, 2 * nyh * nz - 1)]
    arrived(last, z_recv.at[0])
    parts = [S1[yh, z, :, pl.ds(pl.multiple_of(role * (D // 2), D // 2), D // 2)]]
    parts += [RZ[m] for m in range(1, 2 * nyh * nz)]
    while len(parts) > 1:
        parts = [a + b for a, b in zip(parts[::2], parts[1::2])]
    eg_out[...] = parts[0]

    arrived(EB.at[role, my_half], e_send.at[0])
    arrived(EB.at[role, my_half], e_send.at[1])
    arrived(EB.at[role, my_half], e_send.at[2])
    arrived(WX, w_send.at[0])
    arrived(R3V.at[c], r_send.at[0])

    def sent(it):
        if nz > 1:
            arrived(AR1.at[it], a1s.at[it])
        arrived(AR2.at[it], a2s.at[it])

    sent(0)

    @pl.when(teacher)
    def _():
        arrived(ALL, a1s.at[1])
        sent(2)
        for it in range(3):
            for h in range(2):
                arrived(PCS.at[it, h], p_send.at[it, h])
        arrived(UG, u_send.at[0])
        arrived(AR2S, b_send.at[0])

    @pl.when(student)
    def _():
        for k in range(3):
            arrived(SV.at[0], v_send.at[k])

    for m in range(nx):
        arrived(RC.at[pl.ds(0, xrows)], c_send.at[m])
    for h in range(nyh):
        arrived(RX.at[h], x_send.at[h])
    arrived(last, z_send.at[0])
    three = wg_out.at[0, 0, :, pl.ds(0, 3 * PG)]
    arrived(three, g_recv.at[0])
    arrived(three, g_send.at[0])
    mine.wait()


def finish_outputs(wg, eg, wg_out, eg_out):
    wg_out[...] = wg[...]
    eg_out[0] = eg[...].astype(BF16)


def solution(mesh):
    chips = CHIPS[mesh.shape["proto"]]
    nx, nyh, nz = chips

    def per_device(emb, wgt):
        half, D = emb.shape[1:]
        B, PB = 2 * half, wgt.shape[2]
        PC, PG = PB // 2, PB // 4
        vrows, xrows = half // LANES, half // nx
        yrows = xrows // nyh
        owned = yrows // nz
        dma = lambda *shape: pltpu.SemaphoreType.DMA(shape)
        wg, eg = pl.pallas_call(
            functools.partial(kernel, chips),
            name="head_step",
            out_shape=(
                jax.ShapeDtypeStruct((1, 1, D // 4, PB), BF16),
                jax.ShapeDtypeStruct((owned, D // 2), F32),
            ),
            in_specs=[pl.BlockSpec(memory_space=pl.ANY)] * 2,
            out_specs=(pl.BlockSpec(memory_space=pl.ANY), pl.BlockSpec(memory_space=pltpu.VMEM)),
            scratch_shapes=[
                pltpu.VMEM((2, B, D), BF16),
                pltpu.VMEM((D, PB), BF16),
                pltpu.VMEM((D, PG), BF16),
                pltpu.VMEM((half, PB), F32),
                pltpu.VMEM((2, B, PG), F32),
                pltpu.VMEM((B, PG), BF16),
                pltpu.VMEM((D, B), BF16),
                pltpu.VMEM((PG, D), BF16),
                pltpu.VMEM((3, 2, PC // LANES, LANES), F32),
                pltpu.VMEM((3, 2, PC // LANES, LANES), F32),
                pltpu.VMEM((2, PC // LANES, LANES), F32),
                pltpu.VMEM((PG // LANES, LANES), F32),
                pltpu.VMEM((half, LANES), F32),
                pltpu.VMEM((half, LANES), F32),
                pltpu.VMEM((B, LANES), F32),
                pltpu.VMEM((B, LANES), F32),
                pltpu.VMEM((3, vrows, LANES), F32),
                pltpu.VMEM((nx * nyh * nz - 1, vrows, LANES), F32),
                pltpu.VMEM((3, vrows, LANES), F32),
                pltpu.VMEM((3, max(nz - 1, 1), vrows, LANES), F32),
                pltpu.VMEM((3, nx * nyh - 1, vrows, LANES), F32),
                pltpu.VMEM((nx * nyh, vrows, LANES), F32),
                pltpu.VMEM((2, vrows, LANES), F32),
                pltpu.VMEM((2, vrows, LANES), F32),
                pltpu.VMEM((2, half, D), F32),
                pltpu.VMEM((half, D), F32),
                pltpu.VMEM((nyh, nx - 1, yrows, D), F32),
                pltpu.VMEM((nyh, nz, owned, D), F32),
                pltpu.VMEM((2 * nyh * nz, owned, D // 2), F32),
                pltpu.VMEM((D, PG), BF16),
                dma(1), dma(4), dma(3), dma(3), dma(1), dma(1), dma(3, 2), dma(3, 2),
                dma(3), dma(3), dma(3), dma(3), dma(1), dma(1),
                dma(1), dma(1), dma(3), dma(3), dma(1), dma(1), dma(nx), dma(nx), dma(nyh), dma(nyh),
                dma(1), dma(1), dma(1), dma(1), dma(1),
            ],
            compiler_params=pltpu.CompilerParams(
                collective_id=0, has_side_effects=True, vmem_limit_bytes=56 * 1024 * 1024),
            cost_estimate=pl.CostEstimate(
                flops=2 * B * D * PG * 6, bytes_accessed=2 * D * PB, transcendentals=4 * B * PG),
        )(emb, wgt)
        return pl.pallas_call(
            finish_outputs,
            name="outputs",
            out_shape=(
                jax.ShapeDtypeStruct((1, 1, D // 4, PB), BF16),
                jax.ShapeDtypeStruct((1, owned, D // 2), BF16),
            ),
            in_specs=[pl.BlockSpec(memory_space=pltpu.VMEM)] * 2,
            out_specs=(pl.BlockSpec(memory_space=pltpu.VMEM),) * 2,
        )(wg, eg)

    return jax.shard_map(
        per_device,
        mesh=mesh,
        in_specs=(P("role", "crop", None), P("role", None, "proto")),
        out_specs=(P("crop", "role", None, "proto"), P("crop", "proto", "role")),
        check_vma=False,
    )
```

```python
import functools

import jax
import jax.numpy as jnp
from jax import lax
from jax.experimental import pallas as pl
from jax.experimental.pallas import tpu as pltpu
from jax.sharding import PartitionSpec as P

F32 = jnp.float32
BF16 = jnp.bfloat16
MESH = pl.DeviceIdType.MESH
LANES = 128
TILE = 256
CHIPS = {64: (4, 2, 8), 8: (2, 2, 2), 4: (2, 2, 1)}
BATCHES = (5, 6, 5)


def across(column, width):
    return jnp.concatenate([column] * (width // LANES), axis=1)


def far_first(n):
    return sorted(range(1, n), key=lambda m: -max(min(abs(a - (a ^ m)), n - abs(a - (a ^ m))) for a in range(n)))


def kernel(chips, emb, wgt, wg_out, eg_out,
           EB, WO, WX, KC, AB, G, ET, WT, PCS, PCR, UT, UG, RS, COLR, COLS, COL3,
           SRC1, ALL, SRC2, AR1, AR2, AR2S, SV, R3V, EGP, RC, RX, S1, RZ, ZS, ZR, ZX, ZL, WGB,
           loc, w_loc, e_send, e_recv, w_send, w_recv, p_send, p_recv, a1s, a1r, a2s, a2r, b_send, b_recv,
           u_send, u_recv, v_send, v_recv, r_send, r_recv, c_send, c_recv, x_send, x_recv,
           z_send, z_recv, s_send, s_recv, l_send, l_recv, g_send, g_recv, g_loc):
    nx, nyh, nz = chips
    role, p, c = (lax.axis_index(a) for a in ("role", "proto", "crop"))
    x, yh, z = p // (nyh * nz), (p // nz) % nyh, p % nz
    teacher = role == 0
    student = role == 1
    half, D = emb.shape[1], emb.shape[2]
    B = 2 * half
    PB = wgt.shape[2]
    PC, PG = PB // 2, PB // 4
    vrows = half // LANES
    crows, grows = PC // LANES, PG // LANES
    quarter = D // 4

    def at(mr=0, mx=0, my=0, mz=0, mc=0):
        return {"role": role ^ mr, "proto": p ^ ((mx * nyh + my) * nz + mz), "crop": c ^ mc}

    def send(src, dst, s, r, to):
        pltpu.make_async_remote_copy(
            src_ref=src, dst_ref=dst, send_sem=s, recv_sem=r, device_id=to, device_id_type=MESH).start()

    def arrived(ref, sem):
        pltpu.make_async_copy(ref, ref, sem).wait()

    z_peers = far_first(nz)
    x_peers = far_first(nx)
    def hops(m):
        far = 0
        for n, k in ((nx, m // (nyh * nz)), (nz, m % nz)):
            far += max(min(abs(a - (a ^ k)), n - abs(a - (a ^ k))) for a in range(n))
        return far + 2 * ((m // nz) % nyh)

    all_peers = sorted(range(1, nx * nyh * nz), key=lambda m: -hops(m))
    xy_peers = sorted(range(1, nx * nyh), key=lambda m: -((m // nyh in (1, 3)) + 2 * (m // nyh == 2) + 2 * (m % nyh)))

    barrier = pltpu.get_barrier_semaphore()
    greeted = [at(mz=m) for m in z_peers] + [at(mx=m // nyh, my=m % nyh) for m in xy_peers]
    greeted += [at(mr=1, mx=m // nyh, my=m % nyh) for m in range(nx * nyh)] + [at(mc=1), at(mr=1, mc=1)]
    for to in greeted:
        pl.semaphore_signal(barrier, inc=1, device_id=to, device_id_type=MESH)

    my_half = pl.ds(pl.multiple_of(c * half, half), half)
    own_e = pltpu.make_async_copy(emb.at[0], EB.at[role, my_half], loc.at[0])
    own_e.start()
    own_w = []
    for k in range(4):
        cols = pl.ds(k * PG, PG)
        own_w.append(pltpu.make_async_copy(wgt.at[0, :, cols], WO.at[:, cols], w_loc.at[k]))
        own_w[-1].start()

    inv_t, inv_s = 1.0 / 0.07, 1.0 / 0.1
    scale = jnp.where(teacher, inv_t, inv_s).astype(F32)

    own_e.wait()
    for k in range(4):
        own_w[k].wait()

        def own_tile(j, _, k=k):
            cols = pl.ds(pl.multiple_of(k * PG + j * TILE, TILE), TILE)
            s = jnp.dot(EB[role, my_half, :], WO[:, cols], preferred_element_type=F32)
            a = jnp.exp(s * scale)
            KC[:, cols] = a
            cs = jnp.sum(a, axis=0, keepdims=True)
            for l in range(TILE // LANES):
                PCS[0, k // 2, pl.ds((k % 2) * grows + j * (TILE // LANES) + l, 1), :] = cs[:, l * LANES:(l + 1) * LANES]
            return 0

        lax.fori_loop(0, PG // TILE, own_tile, 0)

    S1[:, :, :, D - LANES:] = jnp.zeros(S1.shape[:3] + (LANES,), F32)
    pl.semaphore_wait(barrier, len(greeted))

    g_own = pl.multiple_of(c * PC + role * PG, PG)
    g_away = pl.multiple_of(c * PC + (1 - role) * PG, PG)
    step_rows = D // sum(BATCHES)

    def send_columns(it, h):
        send(PCS.at[it, h], PCR.at[it, h], p_send.at[it, h], p_recv.at[it, h], at(mc=1))

    def send_core():
        send(emb.at[0], EB.at[role, my_half], e_send.at[0], e_recv.at[0], at(mc=1))

    def send_wrap(h):
        rows = pl.ds(h * (half // 2), half // 2)
        there = pl.ds(pl.multiple_of(c * half + h * (half // 2), half // 2), half // 2)
        send(emb.at[0, rows], EB.at[role, there], e_send.at[1], e_recv.at[1], at(mr=1, my=1))

    def send_weights(k):
        for q in range(sum(BATCHES[:k]), sum(BATCHES[:k + 1])):
            rows = pl.ds(q * step_rows, step_rows)
            send(wgt.at[0, rows, pl.ds(g_away, PG)], WX.at[rows, :], w_send.at[0], w_recv.at[0], at(mr=1))

    def expand(vec, ref, first=0):
        for i in range(vrows):
            rows = pl.ds(pl.multiple_of(first + i * LANES, LANES), LANES)
            ref[rows, :] = jnp.broadcast_to(vec[i:i + 1, :], (LANES, LANES)).T

    def column_parts(it, h):
        def body(i, acc):
            for k in range(4):
                rows = pl.ds(pl.multiple_of(i * 32 + k * 8, 8), 8)
                acc = acc + KC[rows, h * PC:(h + 1) * PC] * across(COLR[rows, :], PC)
            return acc

        acc = lax.fori_loop(0, half // 32, body, jnp.zeros((8, PC), F32))
        cs = jnp.sum(acc, axis=0, keepdims=True)
        for l in range(crows):
            PCS[it, h, l:l + 1, :] = cs[:, l * LANES:(l + 1) * LANES]
        send_columns(it, h)

    def column_scales(it, h):
        arrived(PCR.at[it, h], p_recv.at[it, h])
        UT[h] = 1.0 / (PCS[it, h] + PCR[it, h])

    def row_parts(h):
        ub = jnp.concatenate(
            [jnp.broadcast_to(UT[h, l:l + 1, :], (8, LANES)) for l in range(crows)], axis=1)

        def body(i, _):
            for k in range(4):
                rows = pl.ds(pl.multiple_of(i * 32 + k * 8, 8), 8)
                m = KC[rows, h * PC:(h + 1) * PC] * ub
                parts = [m[:, l * LANES:(l + 1) * LANES] for l in range(crows)]
                while len(parts) > 1:
                    parts = [a + b for a, b in zip(parts[::2], parts[1::2])]
                RS[rows, :] = parts[0] if h == 0 else RS[rows, :] + parts[0]
            return 0

        lax.fori_loop(0, half // 32, body, 0)

    def stage1(it):
        for i in range(vrows):
            SRC1[it, i:i + 1, :] = jnp.sum(RS[i * LANES:(i + 1) * LANES, :].T, axis=0, keepdims=True)
        for m in all_peers if it == 1 else z_peers:
            send(SRC1.at[it], ALL.at[m - 1] if it == 1 else AR1.at[it, m - 1], a1s.at[it], a1r.at[it], at(mz=m))

    def stage2(it):
        total = SRC1[it]
        if nz > 1:
            arrived(AR1.at[it], a1r.at[it])
            for m in range(nz - 1):
                total = total + AR1[it, m]
        SRC2[it] = total
        for m in xy_peers:
            send(SRC2.at[it], AR2.at[it, m - 1], a2s.at[it], a2r.at[it], at(mx=m // nyh, my=m % nyh))
        if it == 2:
            for m in range(nx * nyh):
                send(SRC2.at[it], AR2S.at[m], b_send.at[0], b_recv.at[0], at(mr=1, mx=m // nyh, my=m % nyh))

    def finish(it):
        if it == 1:
            arrived(ALL, a1r.at[it])
            parts = [SRC1[it]] + [ALL[m] for m in range(nx * nyh * nz - 1)]
        else:
            arrived(AR2.at[it], a2r.at[it])
            parts = [SRC2[it]] + [AR2[it, m] for m in range(nx * nyh - 1)]
        while len(parts) > 1:
            parts = [a + b for a, b in zip(parts[::2], parts[1::2])]
        return 1.0 / parts[0]

    def forward():
        arrived(EB.at[1 - role, my_half], e_recv.at[1])
        send(EB.at[1 - role, my_half], EB.at[1 - role, my_half], e_send.at[2], e_recv.at[2], at(mc=1))

    def exps(which, weights, first, inv, scaled):
        def tile(j, _):
            cols = pl.ds(pl.multiple_of(j * TILE, TILE), TILE)
            w_cols = pl.ds(pl.multiple_of(first + j * TILE, TILE), TILE)
            s = jnp.dot(EB[which], weights[:, w_cols], preferred_element_type=F32)
            a = jnp.exp(s * inv)
            AB[which, :, cols] = a * across(COLS[...], TILE) if scaled else a
            return 0

        lax.fori_loop(0, PG // TILE, tile, 0)

    def scale_targets():
        ub = jnp.concatenate(
            [jnp.broadcast_to(UG[l:l + 1, :], (8, LANES)) for l in range(grows)], axis=1)

        def body(i, _):
            for k in range(4):
                rows = pl.ds(pl.multiple_of(i * 32 + k * 8, 8), 8)
                AB[0, rows, :] = AB[0, rows, :] * ub
            return 0

        lax.fori_loop(0, B // 32, body, 0)

    def turn_student(weights, first):
        for i in range(B // TILE):
            ET[:, i * TILE:(i + 1) * TILE] = EB[1, i * TILE:(i + 1) * TILE, :].T

        def body(i, _):
            rows = pl.ds(pl.multiple_of(i * TILE, TILE), TILE)
            WT[rows, :] = weights[:, pl.ds(pl.multiple_of(first + i * TILE, TILE), TILE)].T
            return 0

        lax.fori_loop(0, PG // TILE, body, 0)

    @pl.when(teacher)
    def _():
        for h in range(2):
            send_columns(0, h)
        send_core()
        send_wrap(0)
        send_weights(0)
        for h in range(2):
            column_scales(0, h)
            row_parts(h)
        stage1(0)
        arrived(EB.at[role, my_half], e_recv.at[0])
        exps(0, WO, g_own, inv_t, False)
        stage2(0)
        r = finish(0)
        for it in (1, 2):
            expand(r, COLR)
            send_weights(it)
            if it == 1:
                send_wrap(1)
            for h in range(2):
                column_parts(it, h)
            for h in range(2):
                column_scales(it, h)
                row_parts(h)
            stage1(it)
            if it == 2:
                UG[...] = UT[c, 0:grows, :]
                send(UT.at[c, pl.ds(grows, grows)], UG, u_send.at[0], u_recv.at[0], at(mr=1))
                scale_targets()
                arrived(EB.at[1 - role, my_half], e_recv.at[2])
                arrived(WX, w_recv.at[0])
                turn_student(WX, 0)
            if it == 1:
                forward()
            else:
                stage2(it)
                arrived(SV.at[c], v_recv.at[1])
                arrived(SV.at[1 - c], v_recv.at[2])
                for h in range(2):
                    expand(SV[h], COLS, h * half)
                exps(1, WX, 0, inv_s, True)
            r = finish(it)
        R3V[c] = r

    @pl.when(student)
    def _():
        send_core()
        send_wrap(0)
        send_wrap(1)
        send_weights(0)
        for h in range(2):
            UT[h] = jnp.ones((crows, LANES), F32)
            row_parts(h)
        stage1(0)
        stage2(0)
        SV[c] = finish(0)
        send(SV.at[c], SV.at[c], v_send.at[0], v_recv.at[0], at(mc=1))
        send(SV.at[c], SV.at[c], v_send.at[1], v_recv.at[1], at(mr=1))
        send(SV.at[c], SV.at[c], v_send.at[2], v_recv.at[2], at(mr=1, mc=1))
        for k in range(1, len(BATCHES)):
            send_weights(k)
        forward()
        arrived(SV.at[1 - c], v_recv.at[0])
        for h in range(2):
            expand(SV[h], COLS, h * half)
        arrived(EB.at[role, my_half], e_recv.at[0])
        exps(1, WO, g_own, inv_s, True)
        turn_student(WO, g_own)
        arrived(EB.at[1 - role, my_half], e_recv.at[2])
        arrived(WX, w_recv.at[0])
        exps(0, WX, 0, inv_t, False)
        arrived(UG, u_recv.at[0])
        scale_targets()
        arrived(AR2S, b_recv.at[0])
        total = AR2S[0]
        for m in range(1, nx * nyh):
            total = total + AR2S[m]
        R3V[c] = 1.0 / total

    send(R3V.at[c], R3V.at[c], r_send.at[0], r_recv.at[0], at(mc=1))

    xrows = half // nx
    yrows = xrows // nyh
    owned = yrows // nz
    side = half // 2
    blocks = nx // 2
    XC = D - LANES
    x_cols, z_cols = pl.ds(0, XC), pl.ds(XC, LANES)

    def side_rows(h, far):
        return pl.multiple_of(h * half + ((x // blocks) ^ far) * side, side)

    def logit_grads(h, far):
        def body(i, _):
            rows = pl.ds(pl.multiple_of(side_rows(h, far) + i * 16, 16), 16)
            t = AB[0, rows, :] * across(COL3[rows, :], PG)
            G[rows, :] = ((AB[1, rows, :] - t.astype(BF16).astype(F32)) * 10.0).astype(BF16)
            return 0

        lax.fori_loop(0, side // 16, body, 0)

    def embed_parts(h, far):
        rows = pl.ds(side_rows(h, far), side)
        local = pl.ds(pl.multiple_of(((x // blocks) ^ far) * side, side), side)

        def body(j, _):
            cols = pl.ds(pl.multiple_of(j * TILE, TILE), TILE)
            EGP[h, local, cols] = jnp.dot(G[rows, :], WT[:, cols], preferred_element_type=F32)
            return 0

        lax.fori_loop(0, D // TILE, body, 0)

    def x_rows(m):
        return pl.ds(pl.multiple_of((x ^ m) * xrows, xrows), xrows)

    far_side = list(range(blocks, nx))
    near_side = list(range(blocks - 1, -1, -1))

    def send_core_parts(masks):
        for m in masks:
            send(EGP.at[1 - c, x_rows(m)], RC.at[x_rows(m)], c_send.at[m], c_recv.at[m], at(mc=1))

    def send_x_parts(h, masks):
        for m in masks:
            rows = pl.ds(pl.multiple_of((x ^ m) * xrows + h * yrows, yrows), yrows)
            if h == 0:
                arrived(RC.at[x_rows(m)], c_recv.at[m])
            EGP[c, rows, :] = EGP[c, rows, :] + RC[rows, :]
            if m:
                send(EGP.at[c, rows, x_cols], RX.at[h, m - 1], x_send.at[h], x_recv.at[h], at(mx=m))

    expand(R3V[c], COL3, c * half)
    logit_grads(c, 1)
    arrived(R3V.at[1 - c], r_recv.at[0])
    expand(R3V[1 - c], COL3, (1 - c) * half)
    logit_grads(1 - c, 1)
    embed_parts(1 - c, 1)
    send_core_parts(far_side)
    embed_parts(c, 1)
    logit_grads(1 - c, 0)
    embed_parts(1 - c, 0)
    send_core_parts(near_side)
    send_x_parts(0, far_side)
    logit_grads(c, 0)
    embed_parts(c, 0)
    send_x_parts(0, near_side)
    for h in range(1, nyh):
        send_x_parts(h, far_side + near_side)
    for k in range(nx * nyh):
        ZS[:, k] = EGP[c, k * yrows:(k + 1) * yrows, z_cols].reshape(nz, owned, LANES)
    for m in z_peers:
        send(ZS.at[z ^ m], ZR.at[m - 1], s_send.at[0], s_recv.at[0], at(mz=m))

    my_q = 2 * c + role
    out_first = c * PC + role * PG

    def wg_tile(j, _):
        cols = pl.ds(pl.multiple_of(j * TILE, TILE), TILE)
        WGB[:, cols] = jnp.dot(ET[...], G[:, cols], preferred_element_type=F32).astype(BF16)
        dst = wg_out.at[0, 0, :, pl.ds(pl.multiple_of(out_first + j * TILE, TILE), TILE)]
        for m in (1, 3, 2):
            src = WGB.at[pl.ds(pl.multiple_of((my_q ^ m) * quarter, quarter), quarter), cols]
            send(src, dst, g_send.at[0], g_recv.at[0], at(mr=m % 2, mc=m // 2))
        return 0

    lax.fori_loop(0, PG // TILE, wg_tile, 0)
    mine = pltpu.make_async_copy(
        WGB.at[pl.ds(pl.multiple_of(my_q * quarter, quarter), quarter)],
        wg_out.at[0, 0, :, pl.ds(pl.multiple_of(out_first, PG), PG)], g_loc.at[0])
    mine.start()

    total = ZS[z]
    if nz > 1:
        arrived(ZR, s_recv.at[0])
        for m in range(nz - 1):
            total = total + ZR[m]
    ZX[...] = total

    def give_last(mx, yh_to):
        place = ZL.at[(mx * nyh + (yh ^ yh_to)) * 2 + (1 - role)]
        to = {"role": 1, "proto": ((x ^ mx) * nyh + yh_to) * nz + z, "crop": c}
        src = ZX.at[(x ^ mx) * nyh + yh_to]

        def give():
            send(src, place, l_send.at[0], l_recv.at[0], to)

        if mx:
            give()
        else:
            pl.when(jnp.logical_or(teacher, yh != yh_to))(give)

    for m in x_peers + [0]:
        for k in range(nyh):
            give_last(m, k)

    for h in range(nyh):
        rows = pl.ds(pl.multiple_of(x * xrows + h * yrows, yrows), yrows)
        arrived(RX.at[h], x_recv.at[h])
        total = EGP[c, rows, x_cols]
        for m in range(nx - 1):
            total = total + RX[h, m]
        S1[h, :, :, x_cols] = total.reshape(nz, owned, XC)
        my = yh ^ h
        for mz in z_peers + [0]:
            for mr in (1, 0):
                src = S1.at[h, z ^ mz, :, pl.ds(pl.multiple_of((role ^ mr) * (D // 2), D // 2), D // 2)]
                place = RZ.at[(my * 2 + mr) * nz + mz]

                def give(src=src, place=place, mr=mr, mz=mz):
                    send(src, place, z_send.at[0], z_recv.at[0], at(mr=mr, my=my, mz=mz))

                if mr or mz:
                    give()
                else:
                    pl.when(my != 0)(give)
    last = RZ.at[pl.ds(1, 2 * nyh * nz - 1)]
    arrived(last, z_recv.at[0])
    parts = [S1[yh, z, :, pl.ds(pl.multiple_of(role * (D // 2), D // 2), D // 2)]]
    parts += [RZ[m] for m in range(1, 2 * nyh * nz)]
    while len(parts) > 1:
        parts = [a + b for a, b in zip(parts[::2], parts[1::2])]
    eg_out[...] = parts[0]
    others = ZL.at[pl.ds(1, 2 * nx * nyh - 1)]

    @pl.when(student)
    def _():
        arrived(others, l_recv.at[0])
        parts = [ZX[x * nyh + yh]] + [ZL[m] for m in range(1, 2 * nx * nyh)]
        while len(parts) > 1:
            parts = [a + b for a, b in zip(parts[::2], parts[1::2])]
        eg_out[:, D // 2 - LANES:] = parts[0]
        arrived(ZL.at[pl.ds(0, nx * nyh - 1)], l_send.at[0])

    @pl.when(teacher)
    def _():
        arrived(ZL.at[pl.ds(0, nx * nyh)], l_send.at[0])

    if nz > 1:
        arrived(ZR, s_send.at[0])

    arrived(EB.at[role, my_half], e_send.at[0])
    arrived(EB.at[role, my_half], e_send.at[1])
    arrived(EB.at[role, my_half], e_send.at[2])
    arrived(WX, w_send.at[0])
    arrived(R3V.at[c], r_send.at[0])

    def sent(it):
        if nz > 1:
            arrived(AR1.at[it], a1s.at[it])
        arrived(AR2.at[it], a2s.at[it])

    sent(0)

    @pl.when(teacher)
    def _():
        arrived(ALL, a1s.at[1])
        sent(2)
        for it in range(3):
            for h in range(2):
                arrived(PCS.at[it, h], p_send.at[it, h])
        arrived(UG, u_send.at[0])
        arrived(AR2S, b_send.at[0])

    @pl.when(student)
    def _():
        for k in range(3):
            arrived(SV.at[0], v_send.at[k])

    for m in range(nx):
        arrived(RC.at[pl.ds(0, xrows)], c_send.at[m])
    for h in range(nyh):
        arrived(RX.at[h], x_send.at[h])
    arrived(last, z_send.at[0])
    three = wg_out.at[0, 0, :, pl.ds(0, 3 * PG)]
    arrived(three, g_recv.at[0])
    arrived(three, g_send.at[0])
    mine.wait()


def finish_outputs(wg, eg, wg_out, eg_out):
    wg_out[...] = wg[...]
    eg_out[0] = eg[...].astype(BF16)


def solution(mesh):
    chips = CHIPS[mesh.shape["proto"]]
    nx, nyh, nz = chips

    def per_device(emb, wgt):
        half, D = emb.shape[1:]
        B, PB = 2 * half, wgt.shape[2]
        PC, PG = PB // 2, PB // 4
        vrows, xrows = half // LANES, half // nx
        yrows = xrows // nyh
        owned = yrows // nz
        dma = lambda *shape: pltpu.SemaphoreType.DMA(shape)
        wg, eg = pl.pallas_call(
            functools.partial(kernel, chips),
            name="head_step",
            out_shape=(
                jax.ShapeDtypeStruct((1, 1, D // 4, PB), BF16),
                jax.ShapeDtypeStruct((owned, D // 2), F32),
            ),
            in_specs=[pl.BlockSpec(memory_space=pl.ANY)] * 2,
            out_specs=(pl.BlockSpec(memory_space=pl.ANY), pl.BlockSpec(memory_space=pltpu.VMEM)),
            scratch_shapes=[
                pltpu.VMEM((2, B, D), BF16),
                pltpu.VMEM((D, PB), BF16),
                pltpu.VMEM((D, PG), BF16),
                pltpu.VMEM((half, PB), F32),
                pltpu.VMEM((2, B, PG), F32),
                pltpu.VMEM((B, PG), BF16),
                pltpu.VMEM((D, B), BF16),
                pltpu.VMEM((PG, D), BF16),
                pltpu.VMEM((3, 2, PC // LANES, LANES), F32),
                pltpu.VMEM((3, 2, PC // LANES, LANES), F32),
                pltpu.VMEM((2, PC // LANES, LANES), F32),
                pltpu.VMEM((PG // LANES, LANES), F32),
                pltpu.VMEM((half, LANES), F32),
                pltpu.VMEM((half, LANES), F32),
                pltpu.VMEM((B, LANES), F32),
                pltpu.VMEM((B, LANES), F32),
                pltpu.VMEM((3, vrows, LANES), F32),
                pltpu.VMEM((nx * nyh * nz - 1, vrows, LANES), F32),
                pltpu.VMEM((3, vrows, LANES), F32),
                pltpu.VMEM((3, max(nz - 1, 1), vrows, LANES), F32),
                pltpu.VMEM((3, nx * nyh - 1, vrows, LANES), F32),
                pltpu.VMEM((nx * nyh, vrows, LANES), F32),
                pltpu.VMEM((2, vrows, LANES), F32),
                pltpu.VMEM((2, vrows, LANES), F32),
                pltpu.VMEM((2, half, D), F32),
                pltpu.VMEM((half, D), F32),
                pltpu.VMEM((nyh, nx - 1, yrows, D - LANES), F32),
                pltpu.VMEM((nyh, nz, owned, D), F32),
                pltpu.VMEM((2 * nyh * nz, owned, D // 2), F32),
                pltpu.VMEM((nz, nx * nyh, owned, LANES), F32),
                pltpu.VMEM((max(nz - 1, 1), nx * nyh, owned, LANES), F32),
                pltpu.VMEM((nx * nyh, owned, LANES), F32),
                pltpu.VMEM((2 * nx * nyh, owned, LANES), F32),
                pltpu.VMEM((D, PG), BF16),
                dma(1), dma(4), dma(3), dma(3), dma(1), dma(1), dma(3, 2), dma(3, 2),
                dma(3), dma(3), dma(3), dma(3), dma(1), dma(1),
                dma(1), dma(1), dma(3), dma(3), dma(1), dma(1), dma(nx), dma(nx), dma(nyh), dma(nyh),
                dma(1), dma(1), dma(1), dma(1), dma(1), dma(1), dma(1), dma(1), dma(1),
            ],
            compiler_params=pltpu.CompilerParams(
                collective_id=0, has_side_effects=True, vmem_limit_bytes=56 * 1024 * 1024),
            cost_estimate=pl.CostEstimate(
                flops=2 * B * D * PG * 6, bytes_accessed=2 * D * PB, transcendentals=4 * B * PG),
        )(emb, wgt)
        return pl.pallas_call(
            finish_outputs,
            name="outputs",
            out_shape=(
                jax.ShapeDtypeStruct((1, 1, D // 4, PB), BF16),
                jax.ShapeDtypeStruct((1, owned, D // 2), BF16),
            ),
            in_specs=[pl.BlockSpec(memory_space=pltpu.VMEM)] * 2,
            out_specs=(pl.BlockSpec(memory_space=pltpu.VMEM),) * 2,
        )(wg, eg)

    return jax.shard_map(
        per_device,
        mesh=mesh,
        in_specs=(P("role", "crop", None), P("role", None, "proto")),
        out_specs=(P("crop", "role", None, "proto"), P("crop", "proto", "role")),
        check_vma=False,
    )
```

```python
import functools

import jax
import jax.numpy as jnp
from jax import lax
from jax.experimental import pallas as pl
from jax.experimental.pallas import tpu as pltpu
from jax.sharding import PartitionSpec as P

F32 = jnp.float32
BF16 = jnp.bfloat16
MESH = pl.DeviceIdType.MESH
LANES = 128
TILE = 256
CHIPS = {64: (4, 2, 8), 8: (2, 2, 2), 4: (2, 2, 1)}
BATCHES = (5, 6, 5)


def across(column, width):
    return jnp.concatenate([column] * (width // LANES), axis=1)


def far_first(n):
    return sorted(range(1, n), key=lambda m: -max(min(abs(a - (a ^ m)), n - abs(a - (a ^ m))) for a in range(n)))


def kernel(chips, emb, wgt, wg_out, eg_out,
           EB, WO, WX, KC, AB, G, ET, WT, PCS, PCR, UT, UG, RS, COLR, COLS, COL3,
           SRC1, ALL, SRC2, AR1, AR2, AR2S, SV, R3V, EGP, RC, RX, S1, RZ, ZS, ZR, ZX, ZL, WGB,
           loc, w_loc, e_send, e_recv, w_send, w_recv, p_send, p_recv, a1s, a1r, a2s, a2r, b_send, b_recv,
           u_send, u_recv, v_send, v_recv, r_send, r_recv, c_send, c_recv, x_send, x_recv,
           z_send, z_recv, s_send, s_recv, l_send, l_recv, g_send, g_recv, g_loc):
    nx, nyh, nz = chips
    role, p, c = (lax.axis_index(a) for a in ("role", "proto", "crop"))
    x, yh, z = p // (nyh * nz), (p // nz) % nyh, p % nz
    teacher = role == 0
    student = role == 1
    half, D = emb.shape[1], emb.shape[2]
    B = 2 * half
    PB = wgt.shape[2]
    PC, PG = PB // 2, PB // 4
    vrows = half // LANES
    crows, grows = PC // LANES, PG // LANES
    quarter = D // 4

    def at(mr=0, mx=0, my=0, mz=0, mc=0):
        return {"role": role ^ mr, "proto": p ^ ((mx * nyh + my) * nz + mz), "crop": c ^ mc}

    def send(src, dst, s, r, to):
        pltpu.make_async_remote_copy(
            src_ref=src, dst_ref=dst, send_sem=s, recv_sem=r, device_id=to, device_id_type=MESH).start()

    def arrived(ref, sem):
        pltpu.make_async_copy(ref, ref, sem).wait()

    z_peers = far_first(nz)
    x_peers = far_first(nx)
    def hops(m):
        far = 0
        for n, k in ((nx, m // (nyh * nz)), (nz, m % nz)):
            far += max(min(abs(a - (a ^ k)), n - abs(a - (a ^ k))) for a in range(n))
        return far + 2 * ((m // nz) % nyh)

    all_peers = sorted(range(1, nx * nyh * nz), key=lambda m: -hops(m))
    xy_peers = sorted(range(1, nx * nyh), key=lambda m: -((m // nyh in (1, 3)) + 2 * (m // nyh == 2) + 2 * (m % nyh)))

    barrier = pltpu.get_barrier_semaphore()
    greeted = [at(mz=m) for m in z_peers] + [at(mx=m // nyh, my=m % nyh) for m in xy_peers]
    greeted += [at(mr=1, mx=m // nyh, my=m % nyh) for m in range(nx * nyh)] + [at(mc=1), at(mr=1, mc=1)]
    for to in greeted:
        pl.semaphore_signal(barrier, inc=1, device_id=to, device_id_type=MESH)

    my_half = pl.ds(pl.multiple_of(c * half, half), half)
    own_e = pltpu.make_async_copy(emb.at[0], EB.at[role, my_half], loc.at[0])
    own_e.start()
    own_w = []
    for k in range(4):
        cols = pl.ds(k * PG, PG)
        own_w.append(pltpu.make_async_copy(wgt.at[0, :, cols], WO.at[:, cols], w_loc.at[k]))
        own_w[-1].start()

    inv_t, inv_s = 1.0 / 0.07, 1.0 / 0.1
    scale = jnp.where(teacher, inv_t, inv_s).astype(F32)

    own_e.wait()
    for k in range(4):
        own_w[k].wait()

        def own_tile(j, _, k=k):
            cols = pl.ds(pl.multiple_of(k * PG + j * TILE, TILE), TILE)
            s = jnp.dot(EB[role, my_half, :], WO[:, cols], preferred_element_type=F32)
            a = jnp.exp(s * scale)
            KC[:, cols] = a
            cs = jnp.sum(a, axis=0, keepdims=True)
            for l in range(TILE // LANES):
                PCS[0, k // 2, pl.ds((k % 2) * grows + j * (TILE // LANES) + l, 1), :] = cs[:, l * LANES:(l + 1) * LANES]
            return 0

        lax.fori_loop(0, PG // TILE, own_tile, 0)

    S1[:, :, :, D - LANES:] = jnp.zeros(S1.shape[:3] + (LANES,), F32)
    pl.semaphore_wait(barrier, len(greeted))

    g_own = pl.multiple_of(c * PC + role * PG, PG)
    g_away = pl.multiple_of(c * PC + (1 - role) * PG, PG)
    step_rows = D // sum(BATCHES)

    def send_columns(it, h):
        send(PCS.at[it, h], PCR.at[it, h], p_send.at[it, h], p_recv.at[it, h], at(mc=1))

    def send_core():
        send(emb.at[0], EB.at[role, my_half], e_send.at[0], e_recv.at[0], at(mc=1))

    def send_wrap(h):
        rows = pl.ds(h * (half // 2), half // 2)
        there = pl.ds(pl.multiple_of(c * half + h * (half // 2), half // 2), half // 2)
        send(emb.at[0, rows], EB.at[role, there], e_send.at[1], e_recv.at[1], at(mr=1, my=1))

    def send_weights(k):
        for q in range(sum(BATCHES[:k]), sum(BATCHES[:k + 1])):
            rows = pl.ds(q * step_rows, step_rows)
            send(wgt.at[0, rows, pl.ds(g_away, PG)], WX.at[rows, :], w_send.at[0], w_recv.at[0], at(mr=1))

    def expand(vec, ref, first=0):
        for i in range(vrows):
            rows = pl.ds(pl.multiple_of(first + i * LANES, LANES), LANES)
            ref[rows, :] = jnp.broadcast_to(vec[i:i + 1, :], (LANES, LANES)).T

    def column_parts(it, h):
        def body(i, acc):
            for k in range(4):
                rows = pl.ds(pl.multiple_of(i * 32 + k * 8, 8), 8)
                acc = acc + KC[rows, h * PC:(h + 1) * PC] * across(COLR[rows, :], PC)
            return acc

        acc = lax.fori_loop(0, half // 32, body, jnp.zeros((8, PC), F32))
        cs = jnp.sum(acc, axis=0, keepdims=True)
        for l in range(crows):
            PCS[it, h, l:l + 1, :] = cs[:, l * LANES:(l + 1) * LANES]
        send_columns(it, h)

    def column_scales(it, h):
        arrived(PCR.at[it, h], p_recv.at[it, h])
        UT[h] = 1.0 / (PCS[it, h] + PCR[it, h])

    def row_parts(h):
        ub = jnp.concatenate(
            [jnp.broadcast_to(UT[h, l:l + 1, :], (8, LANES)) for l in range(crows)], axis=1)

        def body(i, _):
            for k in range(4):
                rows = pl.ds(pl.multiple_of(i * 32 + k * 8, 8), 8)
                m = KC[rows, h * PC:(h + 1) * PC] * ub
                parts = [m[:, l * LANES:(l + 1) * LANES] for l in range(crows)]
                while len(parts) > 1:
                    parts = [a + b for a, b in zip(parts[::2], parts[1::2])]
                RS[rows, :] = parts[0] if h == 0 else RS[rows, :] + parts[0]
            return 0

        lax.fori_loop(0, half // 32, body, 0)

    def stage1(it):
        for i in range(vrows):
            SRC1[it, i:i + 1, :] = jnp.sum(RS[i * LANES:(i + 1) * LANES, :].T, axis=0, keepdims=True)
        for m in all_peers if it == 1 else z_peers:
            send(SRC1.at[it], ALL.at[m - 1] if it == 1 else AR1.at[it, m - 1], a1s.at[it], a1r.at[it], at(mz=m))

    def stage2(it):
        total = SRC1[it]
        if nz > 1:
            arrived(AR1.at[it], a1r.at[it])
            for m in range(nz - 1):
                total = total + AR1[it, m]
        SRC2[it] = total
        for m in xy_peers:
            send(SRC2.at[it], AR2.at[it, m - 1], a2s.at[it], a2r.at[it], at(mx=m // nyh, my=m % nyh))
        if it == 2:
            for m in range(nx * nyh):
                send(SRC2.at[it], AR2S.at[m], b_send.at[0], b_recv.at[0], at(mr=1, mx=m // nyh, my=m % nyh))

    def finish(it):
        if it == 1:
            arrived(ALL, a1r.at[it])
            parts = [SRC1[it]] + [ALL[m] for m in range(nx * nyh * nz - 1)]
        else:
            arrived(AR2.at[it], a2r.at[it])
            parts = [SRC2[it]] + [AR2[it, m] for m in range(nx * nyh - 1)]
        while len(parts) > 1:
            parts = [a + b for a, b in zip(parts[::2], parts[1::2])]
        return 1.0 / parts[0]

    def forward():
        arrived(EB.at[1 - role, my_half], e_recv.at[1])
        send(EB.at[1 - role, my_half], EB.at[1 - role, my_half], e_send.at[2], e_recv.at[2], at(mc=1))

    def exps(which, weights, first, inv, scaled):
        def tile(j, _):
            cols = pl.ds(pl.multiple_of(j * TILE, TILE), TILE)
            w_cols = pl.ds(pl.multiple_of(first + j * TILE, TILE), TILE)
            s = jnp.dot(EB[which], weights[:, w_cols], preferred_element_type=F32)
            a = jnp.exp(s * inv)
            AB[which, :, cols] = a * across(COLS[...], TILE) if scaled else a
            return 0

        lax.fori_loop(0, PG // TILE, tile, 0)

    def scale_targets():
        ub = jnp.concatenate(
            [jnp.broadcast_to(UG[l:l + 1, :], (8, LANES)) for l in range(grows)], axis=1)

        def body(i, _):
            for k in range(4):
                rows = pl.ds(pl.multiple_of(i * 32 + k * 8, 8), 8)
                AB[0, rows, :] = AB[0, rows, :] * ub
            return 0

        lax.fori_loop(0, B // 32, body, 0)

    def turn_student(weights, first):
        for i in range(B // TILE):
            ET[:, i * TILE:(i + 1) * TILE] = EB[1, i * TILE:(i + 1) * TILE, :].T

        def body(i, _):
            rows = pl.ds(pl.multiple_of(i * TILE, TILE), TILE)
            WT[rows, :] = weights[:, pl.ds(pl.multiple_of(first + i * TILE, TILE), TILE)].T
            return 0

        lax.fori_loop(0, PG // TILE, body, 0)

    @pl.when(teacher)
    def _():
        for h in range(2):
            send_columns(0, h)
        send_core()
        send_wrap(0)
        send_weights(0)
        for h in range(2):
            column_scales(0, h)
            row_parts(h)
        stage1(0)
        arrived(EB.at[role, my_half], e_recv.at[0])
        exps(0, WO, g_own, inv_t, False)
        stage2(0)
        r = finish(0)
        for it in (1, 2):
            expand(r, COLR)
            send_weights(it)
            if it == 1:
                send_wrap(1)
            for h in range(2):
                column_parts(it, h)
            for h in range(2):
                column_scales(it, h)
                row_parts(h)
            stage1(it)
            if it == 2:
                UG[...] = UT[c, 0:grows, :]
                send(UT.at[c, pl.ds(grows, grows)], UG, u_send.at[0], u_recv.at[0], at(mr=1))
                scale_targets()
                arrived(EB.at[1 - role, my_half], e_recv.at[2])
                arrived(WX, w_recv.at[0])
                turn_student(WX, 0)
            if it == 1:
                forward()
            else:
                stage2(it)
                arrived(SV.at[c], v_recv.at[1])
                arrived(SV.at[1 - c], v_recv.at[2])
                for h in range(2):
                    expand(SV[h], COLS, h * half)
                exps(1, WX, 0, inv_s, True)
            r = finish(it)
        R3V[c] = r

    @pl.when(student)
    def _():
        send_core()
        send_wrap(0)
        send_wrap(1)
        send_weights(0)
        for h in range(2):
            UT[h] = jnp.ones((crows, LANES), F32)
            row_parts(h)
        stage1(0)
        stage2(0)
        SV[c] = finish(0)
        send(SV.at[c], SV.at[c], v_send.at[0], v_recv.at[0], at(mc=1))
        send(SV.at[c], SV.at[c], v_send.at[1], v_recv.at[1], at(mr=1))
        send(SV.at[c], SV.at[c], v_send.at[2], v_recv.at[2], at(mr=1, mc=1))
        for k in range(1, len(BATCHES)):
            send_weights(k)
        forward()
        arrived(SV.at[1 - c], v_recv.at[0])
        for h in range(2):
            expand(SV[h], COLS, h * half)
        arrived(EB.at[role, my_half], e_recv.at[0])
        exps(1, WO, g_own, inv_s, True)
        turn_student(WO, g_own)
        arrived(EB.at[1 - role, my_half], e_recv.at[2])
        arrived(WX, w_recv.at[0])
        exps(0, WX, 0, inv_t, False)
        arrived(UG, u_recv.at[0])
        scale_targets()
        arrived(AR2S, b_recv.at[0])
        total = AR2S[0]
        for m in range(1, nx * nyh):
            total = total + AR2S[m]
        R3V[c] = 1.0 / total

    send(R3V.at[c], R3V.at[c], r_send.at[0], r_recv.at[0], at(mc=1))

    xrows = half // nx
    yrows = xrows // nyh
    owned = yrows // nz
    side = half // 2
    blocks = nx // 2
    XC = D - LANES
    x_cols, z_cols = pl.ds(0, XC), pl.ds(XC, LANES)

    def side_rows(h, far):
        return pl.multiple_of(h * half + ((x // blocks) ^ far) * side, side)

    def logit_grads(h, far):
        def body(i, _):
            rows = pl.ds(pl.multiple_of(side_rows(h, far) + i * 16, 16), 16)
            t = AB[0, rows, :] * across(COL3[rows, :], PG)
            G[rows, :] = ((AB[1, rows, :] - t.astype(BF16).astype(F32)) * 10.0).astype(BF16)
            return 0

        lax.fori_loop(0, side // 16, body, 0)

    def embed_parts(h, far):
        rows = pl.ds(side_rows(h, far), side)
        local = pl.ds(pl.multiple_of(((x // blocks) ^ far) * side, side), side)

        def body(j, _):
            cols = pl.ds(pl.multiple_of(j * TILE, TILE), TILE)
            EGP[h, local, cols] = jnp.dot(G[rows, :], WT[:, cols], preferred_element_type=F32)
            return 0

        lax.fori_loop(0, D // TILE, body, 0)

    def x_rows(m):
        return pl.ds(pl.multiple_of((x ^ m) * xrows, xrows), xrows)

    far_side = list(range(blocks, nx))
    near_side = list(range(blocks - 1, -1, -1))

    def send_core_parts(masks):
        for m in masks:
            send(EGP.at[1 - c, x_rows(m)], RC.at[x_rows(m)], c_send.at[m], c_recv.at[m], at(mc=1))

    def send_x_parts(h, masks):
        for m in masks:
            rows = pl.ds(pl.multiple_of((x ^ m) * xrows + h * yrows, yrows), yrows)
            if h == 0:
                arrived(RC.at[x_rows(m)], c_recv.at[m])
            EGP[c, rows, :] = EGP[c, rows, :] + RC[rows, :]
            if m:
                send(EGP.at[c, rows, x_cols], RX.at[h, m - 1], x_send.at[h], x_recv.at[h], at(mx=m))

    expand(R3V[c], COL3, c * half)
    logit_grads(c, 1)
    arrived(R3V.at[1 - c], r_recv.at[0])
    expand(R3V[1 - c], COL3, (1 - c) * half)
    logit_grads(1 - c, 1)
    embed_parts(1 - c, 1)
    send_core_parts(far_side)
    embed_parts(c, 1)
    logit_grads(1 - c, 0)
    embed_parts(1 - c, 0)
    send_core_parts(near_side)
    send_x_parts(0, far_side)
    logit_grads(c, 0)
    embed_parts(c, 0)
    send_x_parts(0, near_side)
    for h in range(1, nyh):
        send_x_parts(h, far_side + near_side)
    for k in range(nx * nyh):
        ZS[:, k] = EGP[c, k * yrows:(k + 1) * yrows, z_cols].reshape(nz, owned, LANES)
    for m in z_peers:
        send(ZS.at[z ^ m], ZR.at[m - 1], s_send.at[0], s_recv.at[0], at(mz=m))

    my_q = 2 * c + role
    out_first = c * PC + role * PG

    def wg_tile(j, _):
        cols = pl.ds(pl.multiple_of(j * TILE, TILE), TILE)
        WGB[:, cols] = jnp.dot(ET[...], G[:, cols], preferred_element_type=F32).astype(BF16)
        dst = wg_out.at[0, 0, :, pl.ds(pl.multiple_of(out_first + j * TILE, TILE), TILE)]
        for m in (1, 3, 2):
            src = WGB.at[pl.ds(pl.multiple_of((my_q ^ m) * quarter, quarter), quarter), cols]
            send(src, dst, g_send.at[0], g_recv.at[0], at(mr=m % 2, mc=m // 2))
        return 0

    lax.fori_loop(0, PG // TILE, wg_tile, 0)
    mine = pltpu.make_async_copy(
        WGB.at[pl.ds(pl.multiple_of(my_q * quarter, quarter), quarter)],
        wg_out.at[0, 0, :, pl.ds(pl.multiple_of(out_first, PG), PG)], g_loc.at[0])
    mine.start()

    total = ZS[z]
    if nz > 1:
        arrived(ZR, s_recv.at[0])
        for m in range(nz - 1):
            total = total + ZR[m]
    ZX[...] = total

    def give_last(mx, yh_to):
        place = ZL.at[(mx * nyh + (yh ^ yh_to)) * 2 + (1 - role)]
        to = {"role": 1, "proto": ((x ^ mx) * nyh + yh_to) * nz + z, "crop": c}
        src = ZX.at[(x ^ mx) * nyh + yh_to]

        def give():
            send(src, place, l_send.at[0], l_recv.at[0], to)

        if mx:
            give()
        else:
            pl.when(jnp.logical_or(teacher, yh != yh_to))(give)

    for m in x_peers + [0]:
        for k in range(nyh):
            give_last(m, k)

    for h in range(nyh):
        rows = pl.ds(pl.multiple_of(x * xrows + h * yrows, yrows), yrows)
        arrived(RX.at[h], x_recv.at[h])
        total = EGP[c, rows, x_cols]
        for m in range(nx - 1):
            total = total + RX[h, m]
        S1[h, :, :, x_cols] = total.reshape(nz, owned, XC)
        my = yh ^ h
        for mz in z_peers + [0]:
            for mr in (1, 0):
                src = S1.at[h, z ^ mz, :, pl.ds(pl.multiple_of((role ^ mr) * (D // 2), D // 2), D // 2)]
                place = RZ.at[(my * 2 + mr) * nz + mz]

                def give(src=src, place=place, mr=mr, mz=mz):
                    send(src, place, z_send.at[0], z_recv.at[0], at(mr=mr, my=my, mz=mz))

                if mr or mz:
                    give()
                else:
                    pl.when(my != 0)(give)
    last = RZ.at[pl.ds(1, 2 * nyh * nz - 1)]
    arrived(last, z_recv.at[0])
    parts = [S1[yh, z, :, pl.ds(pl.multiple_of(role * (D // 2), D // 2), D // 2)]]
    parts += [RZ[m] for m in range(1, 2 * nyh * nz)]
    while len(parts) > 1:
        parts = [a + b for a, b in zip(parts[::2], parts[1::2])]
    eg_out[...] = parts[0]
    others = ZL.at[pl.ds(1, 2 * nx * nyh - 1)]

    @pl.when(student)
    def _():
        arrived(others, l_recv.at[0])
        parts = [ZX[x * nyh + yh]] + [ZL[m] for m in range(1, 2 * nx * nyh)]
        while len(parts) > 1:
            parts = [a + b for a, b in zip(parts[::2], parts[1::2])]
        eg_out[:, D // 2 - LANES:] = parts[0]
        arrived(ZL.at[pl.ds(0, nx * nyh - 1)], l_send.at[0])

    @pl.when(teacher)
    def _():
        arrived(ZL.at[pl.ds(0, nx * nyh)], l_send.at[0])

    if nz > 1:
        arrived(ZR, s_send.at[0])

    arrived(EB.at[role, my_half], e_send.at[0])
    arrived(EB.at[role, my_half], e_send.at[1])
    arrived(EB.at[role, my_half], e_send.at[2])
    arrived(WX, w_send.at[0])
    arrived(R3V.at[c], r_send.at[0])

    def sent(it):
        if nz > 1:
            arrived(AR1.at[it], a1s.at[it])
        arrived(AR2.at[it], a2s.at[it])

    sent(0)

    @pl.when(teacher)
    def _():
        arrived(ALL, a1s.at[1])
        sent(2)
        for it in range(3):
            for h in range(2):
                arrived(PCS.at[it, h], p_send.at[it, h])
        arrived(UG, u_send.at[0])
        arrived(AR2S, b_send.at[0])

    @pl.when(student)
    def _():
        for k in range(3):
            arrived(SV.at[0], v_send.at[k])

    for m in range(nx):
        arrived(RC.at[pl.ds(0, xrows)], c_send.at[m])
    for h in range(nyh):
        arrived(RX.at[h], x_send.at[h])
    arrived(last, z_send.at[0])
    three = wg_out.at[0, 0, :, pl.ds(0, 3 * PG)]
    arrived(three, g_recv.at[0])
    arrived(three, g_send.at[0])
    mine.wait()


def finish_outputs(wg, eg, wg_out, eg_out):
    wg_out[...] = wg[...]
    eg_out[0] = eg[...].astype(BF16)


def solution(mesh):
    chips = CHIPS[mesh.shape["proto"]]
    nx, nyh, nz = chips

    def per_device(emb, wgt):
        half, D = emb.shape[1:]
        B, PB = 2 * half, wgt.shape[2]
        PC, PG = PB // 2, PB // 4
        vrows, xrows = half // LANES, half // nx
        yrows = xrows // nyh
        owned = yrows // nz
        dma = lambda *shape: pltpu.SemaphoreType.DMA(shape)
        wg, eg = pl.pallas_call(
            functools.partial(kernel, chips),
            name="head_step",
            out_shape=(
                jax.ShapeDtypeStruct((1, 1, D // 4, PB), BF16),
                jax.ShapeDtypeStruct((owned, D // 2), F32),
            ),
            in_specs=[pl.BlockSpec(memory_space=pl.ANY)] * 2,
            out_specs=(pl.BlockSpec(memory_space=pl.ANY), pl.BlockSpec(memory_space=pltpu.VMEM)),
            scratch_shapes=[
                pltpu.VMEM((2, B, D), BF16),
                pltpu.VMEM((D, PB), BF16),
                pltpu.VMEM((D, PG), BF16),
                pltpu.VMEM((half, PB), F32),
                pltpu.VMEM((2, B, PG), F32),
                pltpu.VMEM((B, PG), BF16),
                pltpu.VMEM((D, B), BF16),
                pltpu.VMEM((PG, D), BF16),
                pltpu.VMEM((3, 2, PC // LANES, LANES), F32),
                pltpu.VMEM((3, 2, PC // LANES, LANES), F32),
                pltpu.VMEM((2, PC // LANES, LANES), F32),
                pltpu.VMEM((PG // LANES, LANES), F32),
                pltpu.VMEM((half, LANES), F32),
                pltpu.VMEM((half, LANES), F32),
                pltpu.VMEM((B, LANES), F32),
                pltpu.VMEM((B, LANES), F32),
                pltpu.VMEM((3, vrows, LANES), F32),
                pltpu.VMEM((nx * nyh * nz - 1, vrows, LANES), F32),
                pltpu.VMEM((3, vrows, LANES), F32),
                pltpu.VMEM((3, max(nz - 1, 1), vrows, LANES), F32),
                pltpu.VMEM((3, nx * nyh - 1, vrows, LANES), F32),
                pltpu.VMEM((nx * nyh, vrows, LANES), F32),
                pltpu.VMEM((2, vrows, LANES), F32),
                pltpu.VMEM((2, vrows, LANES), F32),
                pltpu.VMEM((2, half, D), F32),
                pltpu.VMEM((half, D), F32),
                pltpu.VMEM((nyh, nx - 1, yrows, D - LANES), F32),
                pltpu.VMEM((nyh, nz, owned, D), F32),
                pltpu.VMEM((2 * nyh * nz, owned, D // 2), F32),
                pltpu.VMEM((nz, nx * nyh, owned, LANES), F32),
                pltpu.VMEM((max(nz - 1, 1), nx * nyh, owned, LANES), F32),
                pltpu.VMEM((nx * nyh, owned, LANES), F32),
                pltpu.VMEM((2 * nx * nyh, owned, LANES), F32),
                pltpu.VMEM((D, PG), BF16),
                dma(1), dma(4), dma(3), dma(3), dma(1), dma(1), dma(3, 2), dma(3, 2),
                dma(3), dma(3), dma(3), dma(3), dma(1), dma(1),
                dma(1), dma(1), dma(3), dma(3), dma(1), dma(1), dma(nx), dma(nx), dma(nyh), dma(nyh),
                dma(1), dma(1), dma(1), dma(1), dma(1), dma(1), dma(1), dma(1), dma(1),
            ],
            compiler_params=pltpu.CompilerParams(
                collective_id=0, has_side_effects=True, vmem_limit_bytes=56 * 1024 * 1024),
            cost_estimate=pl.CostEstimate(
                flops=2 * B * D * PG * 6, bytes_accessed=2 * D * PB, transcendentals=4 * B * PG),
        )(emb, wgt)
        return pl.pallas_call(
            finish_outputs,
            name="outputs",
            out_shape=(
                jax.ShapeDtypeStruct((1, 1, D // 4, PB), BF16),
                jax.ShapeDtypeStruct((1, owned, D // 2), BF16),
            ),
            grid=(2,),
            in_specs=[
                pl.BlockSpec((1, 1, D // 8, PB), lambda k: (0, 0, k, 0)),
                pl.BlockSpec((owned, D // 2), lambda k: (0, 0)),
            ],
            out_specs=(
                pl.BlockSpec((1, 1, D // 8, PB), lambda k: (0, 0, k, 0)),
                pl.BlockSpec((1, owned, D // 2), lambda k: (0, 0, 0)),
            ),
        )(wg, eg)

    return jax.shard_map(
        per_device,
        mesh=mesh,
        in_specs=(P("role", "crop", None), P("role", None, "proto")),
        out_specs=(P("crop", "role", None, "proto"), P("crop", "proto", "role")),
        check_vma=False,
    )
```

```python
import functools

import jax
import jax.numpy as jnp
from jax import lax
from jax.experimental import pallas as pl
from jax.experimental.pallas import tpu as pltpu
from jax.sharding import PartitionSpec as P

F32 = jnp.float32
BF16 = jnp.bfloat16
MESH = pl.DeviceIdType.MESH
LANES = 128
TILE = 256
CHIPS = {64: (4, 2, 8), 8: (2, 2, 2), 4: (2, 2, 1)}
BATCHES = (5, 6, 5)


def across(column, width):
    return jnp.concatenate([column] * (width // LANES), axis=1)


def far_first(n):
    return sorted(range(1, n), key=lambda m: -max(min(abs(a - (a ^ m)), n - abs(a - (a ^ m))) for a in range(n)))


def kernel(chips, emb, wgt, wg_out, eg_out,
           EB, WO, WX, KC, AB, G, ET, WT, PCS, PCR, UT, UG, RS, COLR, COLS, COL3,
           SRC1, ALL, SRC2, AR1, AR2, AR2S, SV, R3V, EGP, RC, RX, S1, RZ, ZS, ZR, ZX, ZL, WGB,
           loc, w_loc, e_send, e_recv, w_send, w_recv, p_send, p_recv, a1s, a1r, a2s, a2r, b_send, b_recv,
           u_send, u_recv, v_send, v_recv, r_send, r_recv, c_send, c_recv, x_send, x_recv,
           z_send, z_recv, s_send, s_recv, l_send, l_recv, g_send, g_recv, g_loc):
    nx, nyh, nz = chips
    role, p, c = (lax.axis_index(a) for a in ("role", "proto", "crop"))
    x, yh, z = p // (nyh * nz), (p // nz) % nyh, p % nz
    teacher = role == 0
    student = role == 1
    half, D = emb.shape[1], emb.shape[2]
    B = 2 * half
    PB = wgt.shape[2]
    PC, PG = PB // 2, PB // 4
    vrows = half // LANES
    crows, grows = PC // LANES, PG // LANES
    quarter = D // 4

    def at(mr=0, mx=0, my=0, mz=0, mc=0):
        return {"role": role ^ mr, "proto": p ^ ((mx * nyh + my) * nz + mz), "crop": c ^ mc}

    def send(src, dst, s, r, to):
        pltpu.make_async_remote_copy(
            src_ref=src, dst_ref=dst, send_sem=s, recv_sem=r, device_id=to, device_id_type=MESH).start()

    def arrived(ref, sem):
        pltpu.make_async_copy(ref, ref, sem).wait()

    z_peers = far_first(nz)
    x_peers = far_first(nx)
    def hops(m):
        far = 0
        for n, k in ((nx, m // (nyh * nz)), (nz, m % nz)):
            far += max(min(abs(a - (a ^ k)), n - abs(a - (a ^ k))) for a in range(n))
        return far + 2 * ((m // nz) % nyh)

    all_peers = sorted(range(1, nx * nyh * nz), key=lambda m: -hops(m))
    xy_peers = sorted(range(1, nx * nyh), key=lambda m: -((m // nyh in (1, 3)) + 2 * (m // nyh == 2) + 2 * (m % nyh)))

    barrier = pltpu.get_barrier_semaphore()
    greeted = [at(mz=m) for m in z_peers] + [at(mx=m // nyh, my=m % nyh) for m in xy_peers]
    greeted += [at(mr=1, mx=m // nyh, my=m % nyh) for m in range(nx * nyh)] + [at(mc=1), at(mr=1, mc=1)]
    for to in greeted:
        pl.semaphore_signal(barrier, inc=1, device_id=to, device_id_type=MESH)

    my_half = pl.ds(pl.multiple_of(c * half, half), half)
    own_e = pltpu.make_async_copy(emb.at[0], EB.at[role, my_half], loc.at[0])
    own_e.start()
    own_w = []
    for k in range(4):
        cols = pl.ds(k * PG, PG)
        own_w.append(pltpu.make_async_copy(wgt.at[0, :, cols], WO.at[:, cols], w_loc.at[k]))
        own_w[-1].start()

    inv_t, inv_s = 1.0 / 0.07, 1.0 / 0.1
    scale = jnp.where(teacher, inv_t, inv_s).astype(F32)

    own_e.wait()
    for k in range(4):
        own_w[k].wait()

        def own_tile(j, _, k=k):
            cols = pl.ds(pl.multiple_of(k * PG + j * TILE, TILE), TILE)
            s = jnp.dot(EB[role, my_half, :], WO[:, cols], preferred_element_type=F32)
            a = jnp.exp(s * scale)
            KC[:, cols] = a
            cs = jnp.sum(a, axis=0, keepdims=True)
            for l in range(TILE // LANES):
                PCS[0, k // 2, pl.ds((k % 2) * grows + j * (TILE // LANES) + l, 1), :] = cs[:, l * LANES:(l + 1) * LANES]
            return 0

        lax.fori_loop(0, PG // TILE, own_tile, 0)

    S1[:, :, :, D - LANES:] = jnp.zeros(S1.shape[:3] + (LANES,), F32)
    pl.semaphore_wait(barrier, len(greeted))

    g_own = pl.multiple_of(c * PC + role * PG, PG)
    g_away = pl.multiple_of(c * PC + (1 - role) * PG, PG)
    step_rows = D // sum(BATCHES)

    def send_columns(it, h):
        send(PCS.at[it, h], PCR.at[it, h], p_send.at[it, h], p_recv.at[it, h], at(mc=1))

    def send_core():
        send(emb.at[0], EB.at[role, my_half], e_send.at[0], e_recv.at[0], at(mc=1))

    def send_wrap(h):
        rows = pl.ds(h * (half // 2), half // 2)
        there = pl.ds(pl.multiple_of(c * half + h * (half // 2), half // 2), half // 2)
        send(emb.at[0, rows], EB.at[role, there], e_send.at[1], e_recv.at[1], at(mr=1, my=1))

    def send_weights(k):
        for q in range(sum(BATCHES[:k]), sum(BATCHES[:k + 1])):
            rows = pl.ds(q * step_rows, step_rows)
            send(wgt.at[0, rows, pl.ds(g_away, PG)], WX.at[rows, :], w_send.at[0], w_recv.at[0], at(mr=1))

    def expand(vec, ref, first=0):
        for i in range(vrows):
            rows = pl.ds(pl.multiple_of(first + i * LANES, LANES), LANES)
            ref[rows, :] = jnp.broadcast_to(vec[i:i + 1, :], (LANES, LANES)).T

    def column_parts(it, h):
        def body(i, acc):
            for k in range(4):
                rows = pl.ds(pl.multiple_of(i * 32 + k * 8, 8), 8)
                acc = acc + KC[rows, h * PC:(h + 1) * PC] * across(COLR[rows, :], PC)
            return acc

        acc = lax.fori_loop(0, half // 32, body, jnp.zeros((8, PC), F32))
        cs = jnp.sum(acc, axis=0, keepdims=True)
        for l in range(crows):
            PCS[it, h, l:l + 1, :] = cs[:, l * LANES:(l + 1) * LANES]
        send_columns(it, h)

    def column_scales(it, h):
        arrived(PCR.at[it, h], p_recv.at[it, h])
        UT[h] = 1.0 / (PCS[it, h] + PCR[it, h])

    def row_parts(h):
        ub = jnp.concatenate(
            [jnp.broadcast_to(UT[h, l:l + 1, :], (8, LANES)) for l in range(crows)], axis=1)

        def body(i, _):
            for k in range(4):
                rows = pl.ds(pl.multiple_of(i * 32 + k * 8, 8), 8)
                m = KC[rows, h * PC:(h + 1) * PC] * ub
                parts = [m[:, l * LANES:(l + 1) * LANES] for l in range(crows)]
                while len(parts) > 1:
                    parts = [a + b for a, b in zip(parts[::2], parts[1::2])]
                RS[rows, :] = parts[0] if h == 0 else RS[rows, :] + parts[0]
            return 0

        lax.fori_loop(0, half // 32, body, 0)

    def stage1(it):
        for i in range(vrows):
            SRC1[it, i:i + 1, :] = jnp.sum(RS[i * LANES:(i + 1) * LANES, :].T, axis=0, keepdims=True)
        for m in all_peers if it == 1 else z_peers:
            send(SRC1.at[it], ALL.at[m - 1] if it == 1 else AR1.at[it, m - 1], a1s.at[it], a1r.at[it], at(mz=m))

    def stage2(it):
        total = SRC1[it]
        if nz > 1:
            arrived(AR1.at[it], a1r.at[it])
            for m in range(nz - 1):
                total = total + AR1[it, m]
        SRC2[it] = total
        for m in xy_peers:
            send(SRC2.at[it], AR2.at[it, m - 1], a2s.at[it], a2r.at[it], at(mx=m // nyh, my=m % nyh))
        if it == 2:
            for m in range(nx * nyh):
                send(SRC2.at[it], AR2S.at[m], b_send.at[0], b_recv.at[0], at(mr=1, mx=m // nyh, my=m % nyh))

    def finish(it):
        if it == 1:
            arrived(ALL, a1r.at[it])
            parts = [SRC1[it]] + [ALL[m] for m in range(nx * nyh * nz - 1)]
        else:
            arrived(AR2.at[it], a2r.at[it])
            parts = [SRC2[it]] + [AR2[it, m] for m in range(nx * nyh - 1)]
        while len(parts) > 1:
            parts = [a + b for a, b in zip(parts[::2], parts[1::2])]
        return 1.0 / parts[0]

    def forward():
        arrived(EB.at[1 - role, my_half], e_recv.at[1])
        send(EB.at[1 - role, my_half], EB.at[1 - role, my_half], e_send.at[2], e_recv.at[2], at(mc=1))

    def exps(which, weights, first, inv, scaled):
        def tile(j, _):
            cols = pl.ds(pl.multiple_of(j * TILE, TILE), TILE)
            w_cols = pl.ds(pl.multiple_of(first + j * TILE, TILE), TILE)
            s = jnp.dot(EB[which], weights[:, w_cols], preferred_element_type=F32)
            a = jnp.exp(s * inv)
            AB[which, :, cols] = a * across(COLS[...], TILE) if scaled else a
            return 0

        lax.fori_loop(0, PG // TILE, tile, 0)

    def scale_targets():
        ub = jnp.concatenate(
            [jnp.broadcast_to(UG[l:l + 1, :], (8, LANES)) for l in range(grows)], axis=1)

        def body(i, _):
            for k in range(4):
                rows = pl.ds(pl.multiple_of(i * 32 + k * 8, 8), 8)
                AB[0, rows, :] = AB[0, rows, :] * ub
            return 0

        lax.fori_loop(0, B // 32, body, 0)

    def turn_student(weights, first):
        for i in range(B // TILE):
            ET[:, i * TILE:(i + 1) * TILE] = EB[1, i * TILE:(i + 1) * TILE, :].T

        def body(i, _):
            rows = pl.ds(pl.multiple_of(i * TILE, TILE), TILE)
            WT[rows, :] = weights[:, pl.ds(pl.multiple_of(first + i * TILE, TILE), TILE)].T
            return 0

        lax.fori_loop(0, PG // TILE, body, 0)

    @pl.when(teacher)
    def _():
        for h in range(2):
            send_columns(0, h)
        send_core()
        send_wrap(0)
        send_weights(0)
        for h in range(2):
            column_scales(0, h)
            row_parts(h)
        stage1(0)
        arrived(EB.at[role, my_half], e_recv.at[0])
        exps(0, WO, g_own, inv_t, False)
        stage2(0)
        r = finish(0)
        for it in (1, 2):
            expand(r, COLR)
            send_weights(it)
            if it == 1:
                send_wrap(1)
            for h in range(2):
                column_parts(it, h)
            for h in range(2):
                column_scales(it, h)
                row_parts(h)
            stage1(it)
            if it == 2:
                UG[...] = UT[c, 0:grows, :]
                send(UT.at[c, pl.ds(grows, grows)], UG, u_send.at[0], u_recv.at[0], at(mr=1))
                scale_targets()
                arrived(EB.at[1 - role, my_half], e_recv.at[2])
                arrived(WX, w_recv.at[0])
                turn_student(WX, 0)
            if it == 1:
                forward()
            else:
                stage2(it)
                arrived(SV.at[c], v_recv.at[1])
                arrived(SV.at[1 - c], v_recv.at[2])
                for h in range(2):
                    expand(SV[h], COLS, h * half)
                exps(1, WX, 0, inv_s, True)
            r = finish(it)
        R3V[c] = r

    @pl.when(student)
    def _():
        send_core()
        send_wrap(0)
        send_wrap(1)
        send_weights(0)
        for h in range(2):
            UT[h] = jnp.ones((crows, LANES), F32)
            row_parts(h)
        stage1(0)
        stage2(0)
        SV[c] = finish(0)
        send(SV.at[c], SV.at[c], v_send.at[0], v_recv.at[0], at(mc=1))
        send(SV.at[c], SV.at[c], v_send.at[1], v_recv.at[1], at(mr=1))
        send(SV.at[c], SV.at[c], v_send.at[2], v_recv.at[2], at(mr=1, mc=1))
        for k in range(1, len(BATCHES)):
            send_weights(k)
        forward()
        arrived(SV.at[1 - c], v_recv.at[0])
        for h in range(2):
            expand(SV[h], COLS, h * half)
        arrived(EB.at[role, my_half], e_recv.at[0])
        exps(1, WO, g_own, inv_s, True)
        turn_student(WO, g_own)
        arrived(EB.at[1 - role, my_half], e_recv.at[2])
        arrived(WX, w_recv.at[0])
        exps(0, WX, 0, inv_t, False)
        arrived(UG, u_recv.at[0])
        scale_targets()
        arrived(AR2S, b_recv.at[0])
        total = AR2S[0]
        for m in range(1, nx * nyh):
            total = total + AR2S[m]
        R3V[c] = 1.0 / total

    send(R3V.at[c], R3V.at[c], r_send.at[0], r_recv.at[0], at(mc=1))

    xrows = half // nx
    yrows = xrows // nyh
    owned = yrows // nz
    side = half // 2
    blocks = nx // 2
    XC = D - LANES
    x_cols, z_cols = pl.ds(0, XC), pl.ds(XC, LANES)

    def side_rows(h, far):
        return pl.multiple_of(h * half + ((x // blocks) ^ far) * side, side)

    def logit_grads(h, far):
        def body(i, _):
            rows = pl.ds(pl.multiple_of(side_rows(h, far) + i * 16, 16), 16)
            t = AB[0, rows, :] * across(COL3[rows, :], PG)
            G[rows, :] = ((AB[1, rows, :] - t.astype(BF16).astype(F32)) * 10.0).astype(BF16)
            return 0

        lax.fori_loop(0, side // 16, body, 0)

    def embed_parts(h, far):
        rows = pl.ds(side_rows(h, far), side)
        local = pl.ds(pl.multiple_of(((x // blocks) ^ far) * side, side), side)

        EGP[h, local, :] = jnp.dot(G[rows, :], WT[...], preferred_element_type=F32)

    def x_rows(m):
        return pl.ds(pl.multiple_of((x ^ m) * xrows, xrows), xrows)

    far_side = list(range(blocks, nx))
    near_side = list(range(blocks - 1, -1, -1))

    def send_core_parts(masks):
        for m in masks:
            send(EGP.at[1 - c, x_rows(m)], RC.at[x_rows(m)], c_send.at[m], c_recv.at[m], at(mc=1))

    def send_x_parts(h, masks):
        for m in masks:
            rows = pl.ds(pl.multiple_of((x ^ m) * xrows + h * yrows, yrows), yrows)
            if h == 0:
                arrived(RC.at[x_rows(m)], c_recv.at[m])
            EGP[c, rows, :] = EGP[c, rows, :] + RC[rows, :]
            if m:
                send(EGP.at[c, rows, x_cols], RX.at[h, m - 1], x_send.at[h], x_recv.at[h], at(mx=m))

    expand(R3V[c], COL3, c * half)
    logit_grads(c, 1)
    arrived(R3V.at[1 - c], r_recv.at[0])
    expand(R3V[1 - c], COL3, (1 - c) * half)
    logit_grads(1 - c, 1)
    embed_parts(1 - c, 1)
    send_core_parts(far_side)
    embed_parts(c, 1)
    logit_grads(1 - c, 0)
    embed_parts(1 - c, 0)
    send_core_parts(near_side)
    send_x_parts(0, far_side)
    logit_grads(c, 0)
    embed_parts(c, 0)
    send_x_parts(0, near_side)
    for h in range(1, nyh):
        send_x_parts(h, far_side + near_side)
    for k in range(nx * nyh):
        ZS[:, k] = EGP[c, k * yrows:(k + 1) * yrows, z_cols].reshape(nz, owned, LANES)
    for m in z_peers:
        send(ZS.at[z ^ m], ZR.at[m - 1], s_send.at[0], s_recv.at[0], at(mz=m))

    my_q = 2 * c + role
    out_first = c * PC + role * PG

    def wg_tile(j, _):
        cols = pl.ds(pl.multiple_of(j * TILE, TILE), TILE)
        WGB[:, cols] = jnp.dot(ET[...], G[:, cols], preferred_element_type=F32).astype(BF16)
        dst = wg_out.at[0, 0, :, pl.ds(pl.multiple_of(out_first + j * TILE, TILE), TILE)]
        for m in (1, 3, 2):
            src = WGB.at[pl.ds(pl.multiple_of((my_q ^ m) * quarter, quarter), quarter), cols]
            send(src, dst, g_send.at[0], g_recv.at[0], at(mr=m % 2, mc=m // 2))
        return 0

    lax.fori_loop(0, PG // TILE, wg_tile, 0)
    mine = pltpu.make_async_copy(
        WGB.at[pl.ds(pl.multiple_of(my_q * quarter, quarter), quarter)],
        wg_out.at[0, 0, :, pl.ds(pl.multiple_of(out_first, PG), PG)], g_loc.at[0])
    mine.start()

    total = ZS[z]
    if nz > 1:
        arrived(ZR, s_recv.at[0])
        for m in range(nz - 1):
            total = total + ZR[m]
    ZX[...] = total

    def give_last(mx, yh_to):
        place = ZL.at[(mx * nyh + (yh ^ yh_to)) * 2 + (1 - role)]
        to = {"role": 1, "proto": ((x ^ mx) * nyh + yh_to) * nz + z, "crop": c}
        src = ZX.at[(x ^ mx) * nyh + yh_to]

        def give():
            send(src, place, l_send.at[0], l_recv.at[0], to)

        if mx:
            give()
        else:
            pl.when(jnp.logical_or(teacher, yh != yh_to))(give)

    for m in x_peers + [0]:
        for k in range(nyh):
            give_last(m, k)

    for h in range(nyh):
        rows = pl.ds(pl.multiple_of(x * xrows + h * yrows, yrows), yrows)
        arrived(RX.at[h], x_recv.at[h])
        total = EGP[c, rows, x_cols]
        for m in range(nx - 1):
            total = total + RX[h, m]
        S1[h, :, :, x_cols] = total.reshape(nz, owned, XC)
        my = yh ^ h
        for mz in z_peers + [0]:
            for mr in (1, 0):
                src = S1.at[h, z ^ mz, :, pl.ds(pl.multiple_of((role ^ mr) * (D // 2), D // 2), D // 2)]
                place = RZ.at[(my * 2 + mr) * nz + mz]

                def give(src=src, place=place, mr=mr, mz=mz):
                    send(src, place, z_send.at[0], z_recv.at[0], at(mr=mr, my=my, mz=mz))

                if mr or mz:
                    give()
                else:
                    pl.when(my != 0)(give)
    last = RZ.at[pl.ds(1, 2 * nyh * nz - 1)]
    arrived(last, z_recv.at[0])
    parts = [S1[yh, z, :, pl.ds(pl.multiple_of(role * (D // 2), D // 2), D // 2)]]
    parts += [RZ[m] for m in range(1, 2 * nyh * nz)]
    while len(parts) > 1:
        parts = [a + b for a, b in zip(parts[::2], parts[1::2])]
    eg_out[...] = parts[0]
    others = ZL.at[pl.ds(1, 2 * nx * nyh - 1)]

    @pl.when(student)
    def _():
        arrived(others, l_recv.at[0])
        parts = [ZX[x * nyh + yh]] + [ZL[m] for m in range(1, 2 * nx * nyh)]
        while len(parts) > 1:
            parts = [a + b for a, b in zip(parts[::2], parts[1::2])]
        eg_out[:, D // 2 - LANES:] = parts[0]
        arrived(ZL.at[pl.ds(0, nx * nyh - 1)], l_send.at[0])

    @pl.when(teacher)
    def _():
        arrived(ZL.at[pl.ds(0, nx * nyh)], l_send.at[0])

    if nz > 1:
        arrived(ZR, s_send.at[0])

    arrived(EB.at[role, my_half], e_send.at[0])
    arrived(EB.at[role, my_half], e_send.at[1])
    arrived(EB.at[role, my_half], e_send.at[2])
    arrived(WX, w_send.at[0])
    arrived(R3V.at[c], r_send.at[0])

    def sent(it):
        if nz > 1:
            arrived(AR1.at[it], a1s.at[it])
        arrived(AR2.at[it], a2s.at[it])

    sent(0)

    @pl.when(teacher)
    def _():
        arrived(ALL, a1s.at[1])
        sent(2)
        for it in range(3):
            for h in range(2):
                arrived(PCS.at[it, h], p_send.at[it, h])
        arrived(UG, u_send.at[0])
        arrived(AR2S, b_send.at[0])

    @pl.when(student)
    def _():
        for k in range(3):
            arrived(SV.at[0], v_send.at[k])

    for m in range(nx):
        arrived(RC.at[pl.ds(0, xrows)], c_send.at[m])
    for h in range(nyh):
        arrived(RX.at[h], x_send.at[h])
    arrived(last, z_send.at[0])
    three = wg_out.at[0, 0, :, pl.ds(0, 3 * PG)]
    arrived(three, g_recv.at[0])
    arrived(three, g_send.at[0])
    mine.wait()


def finish_outputs(wg, eg, wg_out, eg_out):
    wg_out[...] = wg[...]
    eg_out[0] = eg[...].astype(BF16)


def solution(mesh):
    chips = CHIPS[mesh.shape["proto"]]
    nx, nyh, nz = chips

    def per_device(emb, wgt):
        half, D = emb.shape[1:]
        B, PB = 2 * half, wgt.shape[2]
        PC, PG = PB // 2, PB // 4
        vrows, xrows = half // LANES, half // nx
        yrows = xrows // nyh
        owned = yrows // nz
        dma = lambda *shape: pltpu.SemaphoreType.DMA(shape)
        wg, eg = pl.pallas_call(
            functools.partial(kernel, chips),
            name="head_step",
            out_shape=(
                jax.ShapeDtypeStruct((1, 1, D // 4, PB), BF16),
                jax.ShapeDtypeStruct((owned, D // 2), F32),
            ),
            in_specs=[pl.BlockSpec(memory_space=pl.ANY)] * 2,
            out_specs=(pl.BlockSpec(memory_space=pl.ANY), pl.BlockSpec(memory_space=pltpu.VMEM)),
            scratch_shapes=[
                pltpu.VMEM((2, B, D), BF16),
                pltpu.VMEM((D, PB), BF16),
                pltpu.VMEM((D, PG), BF16),
                pltpu.VMEM((half, PB), F32),
                pltpu.VMEM((2, B, PG), F32),
                pltpu.VMEM((B, PG), BF16),
                pltpu.VMEM((D, B), BF16),
                pltpu.VMEM((PG, D), BF16),
                pltpu.VMEM((3, 2, PC // LANES, LANES), F32),
                pltpu.VMEM((3, 2, PC // LANES, LANES), F32),
                pltpu.VMEM((2, PC // LANES, LANES), F32),
                pltpu.VMEM((PG // LANES, LANES), F32),
                pltpu.VMEM((half, LANES), F32),
                pltpu.VMEM((half, LANES), F32),
                pltpu.VMEM((B, LANES), F32),
                pltpu.VMEM((B, LANES), F32),
                pltpu.VMEM((3, vrows, LANES), F32),
                pltpu.VMEM((nx * nyh * nz - 1, vrows, LANES), F32),
                pltpu.VMEM((3, vrows, LANES), F32),
                pltpu.VMEM((3, max(nz - 1, 1), vrows, LANES), F32),
                pltpu.VMEM((3, nx * nyh - 1, vrows, LANES), F32),
                pltpu.VMEM((nx * nyh, vrows, LANES), F32),
                pltpu.VMEM((2, vrows, LANES), F32),
                pltpu.VMEM((2, vrows, LANES), F32),
                pltpu.VMEM((2, half, D), F32),
                pltpu.VMEM((half, D), F32),
                pltpu.VMEM((nyh, nx - 1, yrows, D - LANES), F32),
                pltpu.VMEM((nyh, nz, owned, D), F32),
                pltpu.VMEM((2 * nyh * nz, owned, D // 2), F32),
                pltpu.VMEM((nz, nx * nyh, owned, LANES), F32),
                pltpu.VMEM((max(nz - 1, 1), nx * nyh, owned, LANES), F32),
                pltpu.VMEM((nx * nyh, owned, LANES), F32),
                pltpu.VMEM((2 * nx * nyh, owned, LANES), F32),
                pltpu.VMEM((D, PG), BF16),
                dma(1), dma(4), dma(3), dma(3), dma(1), dma(1), dma(3, 2), dma(3, 2),
                dma(3), dma(3), dma(3), dma(3), dma(1), dma(1),
                dma(1), dma(1), dma(3), dma(3), dma(1), dma(1), dma(nx), dma(nx), dma(nyh), dma(nyh),
                dma(1), dma(1), dma(1), dma(1), dma(1), dma(1), dma(1), dma(1), dma(1),
            ],
            compiler_params=pltpu.CompilerParams(
                collective_id=0, has_side_effects=True, vmem_limit_bytes=56 * 1024 * 1024),
            cost_estimate=pl.CostEstimate(
                flops=2 * B * D * PG * 6, bytes_accessed=2 * D * PB, transcendentals=4 * B * PG),
        )(emb, wgt)
        return pl.pallas_call(
            finish_outputs,
            name="outputs",
            out_shape=(
                jax.ShapeDtypeStruct((1, 1, D // 4, PB), BF16),
                jax.ShapeDtypeStruct((1, owned, D // 2), BF16),
            ),
            grid=(2,),
            in_specs=[
                pl.BlockSpec((1, 1, D // 8, PB), lambda k: (0, 0, k, 0)),
                pl.BlockSpec((owned, D // 2), lambda k: (0, 0)),
            ],
            out_specs=(
                pl.BlockSpec((1, 1, D // 8, PB), lambda k: (0, 0, k, 0)),
                pl.BlockSpec((1, owned, D // 2), lambda k: (0, 0, 0)),
            ),
        )(wg, eg)

    return jax.shard_map(
        per_device,
        mesh=mesh,
        in_specs=(P("role", "crop", None), P("role", None, "proto")),
        out_specs=(P("crop", "role", None, "proto"), P("crop", "proto", "role")),
        check_vma=False,
    )
```
